128 devices in a mesh: dp: 8 (over x, core), fsdp: 16 (over y, z).
Axes of the slice: x: 4, y: 4, z: 4, core: 2. Of those that a mesh axis runs over, the one named last changes fastest.
Arguments:
- grad_parts: bfloat16 [8, 8192, 14336], P('dp', 'fsdp'), may hold values from -8 to 8
- weight: bfloat16 [8192, 14336], P('fsdp', 'dp'), may hold values from -6 to 6
- projector: float32 [8192, 512], P('fsdp'), may hold values from -0.0625 to 0.0625
- exp_avg: float32 [512, 14336], P('fsdp', 'dp'), may hold values from -4 to 4
- exp_avg_sq: float32 [512, 14336], P('fsdp', 'dp'), may hold values from 0.1 to 1
Outputs:
- new_weight: bfloat16 [8192, 14336], P('fsdp', 'dp')
- new_projector: float32 [8192, 512], P('fsdp')
- moment_one: float32 [512, 14336], P('fsdp', 'dp')
- moment_two: float32 [512, 14336], P('fsdp', 'dp')
The draws below stay inside these ranges and needn't reach their ends.
All inputs are finite; a program needn't handle non-finite values.
Results may differ from the reference program's by a relative error of at most 0.009.
Values may be sent and summed in bfloat16 or wider, within the bound.
A program may use at most 128 MiB of HBM per device.

```python
import math
import jax
import jax.numpy as jnp
from jax import lax

D = 8192
FF = 14336
R = 512
NS_ITERS = 5
N_DP = 8


def grad_entries(key, rise):
    key_vals, key_pair = jax.random.split(key)
    values = jnp.clip(jax.random.normal(key_vals, (N_DP, D, FF), jnp.float32), -6.0, 6.0)
    position = jnp.arange(D, dtype=jnp.float32) / jnp.float32(max(D - 1, 1))
    log_rise = math.log(rise)
    mean_square = (rise * rise - 1.0) / (2.0 * log_rise)
    row_scale = jnp.exp(log_rise * position) / math.sqrt(mean_square)
    pairing = jax.random.permutation(key_pair, N_DP)
    block_of = jnp.arange(FF, dtype=jnp.int32) // (FF // N_DP)
    owner = pairing[block_of]
    replica = jnp.arange(N_DP, dtype=jnp.int32)
    spike = jnp.where(replica[:, None] == owner[None, :], 3.0, 1.0).astype(jnp.float32)
    full = 0.35 * values * row_scale[None, :, None] * spike[:, None, :]
    return jnp.clip(full, -8.0, 8.0).astype(jnp.bfloat16)


def draw_grad_parts(key, part):
    key = jax.random.fold_in(key, 11)
    return grad_entries(key, 10.0)


def level_of(stream_key, dims, cuts, smallest, high):
    loudness = 1.0
    for axis_at, shards_of in cuts:
        draws = jax.random.uniform(jax.random.fold_in(jax.random.fold_in(stream_key, 6), axis_at), (shards_of,), jnp.float32, smallest / len(cuts), high / len(cuts))
        loudness = loudness * jnp.repeat(jnp.exp(draws), dims[axis_at] // shards_of).reshape((-1,) + (1,) * (len(dims) - 1 - axis_at))
    return loudness


def centred(own_key, shape, deviation, most, cuts=(), kind=jnp.bfloat16):
    result = jax.random.normal(own_key, shape, jnp.float32) * deviation
    if len(cuts) > 0:
        result = level_of(own_key, shape, cuts, -0.22, 0.18) * result
    return jnp.clip(result, min=-most, max=most).astype(kind)


def setup_inputs(seed: int = 0) -> dict:
    key_of = jax.random.split(jax.random.key(seed), 6)
    grad_parts = draw_grad_parts(jax.random.fold_in(key_of[5], 71), 0)
    weight = centred(key_of[1], (D, FF), 1.0, 6.0, ((0, 16), (1, 8)))
    projector = centred(key_of[2], (D, R), D ** -0.5, 0.0625, ((0, 16),), jnp.float32)
    exp_avg = centred(key_of[3], (R, FF), 0.3, 4.0, ((0, 16), (1, 8)), jnp.float32)
    exp_avg_sq = jnp.clip(jnp.exp(math.log(1.0) - 2.3025851 * jax.random.uniform(key_of[4], (R, FF), jnp.float32) ** level_of(key_of[4], (R, FF), ((0, 16), (1, 8)), -0.2, 0.2)), 0.1, 1.0)
    return dict(grad_parts=grad_parts, weight=weight, projector=projector, exp_avg=exp_avg, exp_avg_sq=exp_avg_sq)


COEF_A = 3.4445
COEF_B = -4.775
COEF_C = 2.0315

def reference(grad_parts, weight, projector, exp_avg, exp_avg_sq):
    highest = lax.Precision.HIGHEST
    grad_total = grad_parts[0].astype(jnp.float32)
    for replica in range(1, N_DP):
        grad_total = grad_total + grad_parts[replica].astype(jnp.float32)
    low_rank = jnp.dot(projector.T, grad_total, precision=highest, preferred_element_type=jnp.float32)
    moment_one = 0.9 * exp_avg + 0.1 * low_rank
    moment_two = 0.999 * exp_avg_sq + 0.001 * low_rank * low_rank
    normed = moment_one / (jnp.sqrt(moment_two) + 1e-08)
    update = jnp.dot(projector, normed, precision=highest, preferred_element_type=jnp.float32)
    new_weight = (weight.astype(jnp.float32) - 2.0 * update).astype(jnp.bfloat16)
    residual = grad_total - jnp.dot(projector, low_rank, precision=highest, preferred_element_type=jnp.float32)
    tangent = jnp.dot(residual, low_rank.T, precision=highest, preferred_element_type=jnp.float32)
    tan_scale = 0.5 * jnp.sqrt(jnp.float32(R)) / jnp.sqrt(jnp.sum(tangent * tangent) + 1e-06)
    frame = projector + tan_scale * tangent
    frame_iter = frame / jnp.sqrt(jnp.sum(frame * frame) + 1e-06)
    identity = jnp.eye(R, dtype=jnp.float32)
    for sweep in range(NS_ITERS):
        gram = jnp.dot(frame_iter.T, frame_iter, precision=highest, preferred_element_type=jnp.float32)
        squared = jnp.dot(gram, gram, precision=highest, preferred_element_type=jnp.float32)
        polynomial = COEF_A * identity + COEF_B * gram + COEF_C * squared
        frame_iter = jnp.dot(frame_iter, polynomial, precision=highest, preferred_element_type=jnp.float32)
    return (new_weight, frame_iter, moment_one, moment_two)
```

```python
import jax
import jax.numpy as jnp
from jax import lax
from jax.experimental import pallas as pl
from jax.experimental.pallas import tpu as pltpu
from jax.sharding import PartitionSpec as P

NS_ITERS = 5

COEF_A = 3.4445
COEF_B = -4.775
COEF_C = 2.0315

MESH = pl.DeviceIdType.MESH
BF16 = jnp.bfloat16
F32 = jnp.float32

N_X = 4
N_DP = 8
N_FSDP = 16
CHUNK = 256
AHEAD = 3


def dot(left, right):
    return jnp.dot(left, right, preferred_element_type=F32)


def dot_nt(left, right):
    return lax.dot_general(left, right, (((1,), (1,)), ((), ())), preferred_element_type=F32)


def split(value):
    high = value.astype(BF16)
    return high, (value - high.astype(F32)).astype(BF16)


def dot3(left, right):
    return dot(left[0], right[0]) + dot(left[0], right[1]) + dot(left[1], right[0])


def diagonal(shape, row_at, col_at):
    rows = lax.broadcasted_iota(jnp.int32, shape, 0) + row_at
    cols = lax.broadcasted_iota(jnp.int32, shape, 1) + col_at
    return rows == cols


def fold_rows(value):
    rows, cols = value.shape
    part = jnp.sum(value.reshape(rows // 8, 8, cols), axis=0)
    total = part[:, 0:128]
    for at in range(128, cols, 128):
        total = total + part[:, at : at + 128]
    return total


def kernel(
    grad, weight, proj, avg, avg_sq,
    new_weight, new_proj, moment_one, moment_two,
    own, sib_in, opp_top, opp_bot, from_m, from_p,
    low_part, low_in, low_norm,
    w_buf, p_buf, m_buf, v_buf, p_bf, p_t, tan_acc,
    tan_send, tan_in, tan_all, gram_send, gram_in, gram_all,
    gram_buf, q_buf, out_buf,
    load_sem, own_sem, sib_ssem, sib_rsem, x_ssem, x_rsem,
    low_ssem, low_rsem, ln_ssem, ln_rsem, tail_ssem, tail_rsem, out_sem,
):
    rows = grad.shape[0]
    rank = proj.shape[1]
    share = avg.shape[0]
    owned = avg.shape[1]
    steps = owned // CHUNK
    half = rows // 2
    tan_rows = rank // N_DP

    d = lax.axis_index("dp")
    f = lax.axis_index("fsdp")
    x = d // 2
    core = d % 2
    sib = 2 * x + (1 - core)
    right = 2 * ((x + 1) % N_X) + core
    left = 2 * ((x + 3) % N_X) + core

    def remote(src, dst, ssem, rsem, device):
        return pltpu.make_async_remote_copy(
            src_ref=src, dst_ref=dst, send_sem=ssem, recv_sem=rsem, device_id=device, device_id_type=MESH
        )

    def columns(owner, j):
        return pl.ds(pl.multiple_of(owner * owned + j * CHUNK, CHUNK), CHUNK)

    def step_columns(j):
        return pl.ds(pl.multiple_of(j * CHUNK, CHUNK), CHUNK)

    def own_copy(q, j):
        return pltpu.make_async_copy(
            grad.at[:, columns(2 * ((x + q) % N_X) + core, j)], own.at[q, j], own_sem.at[j, q]
        )

    def sib_copy(q, j):
        return remote(
            grad.at[:, columns(2 * ((x + q) % N_X) + (1 - core), j)],
            sib_in.at[q, j], sib_ssem.at[j, q], sib_rsem.at[j, q], {"dp": sib},
        )

    top, bot = pl.ds(0, half), pl.ds(half, half)

    def x_copy(k, j):
        src, dst, device = (
            (lambda: (own.at[2, j, top], opp_top.at[j], right)),
            (lambda: (own.at[2, j, bot], opp_bot.at[j], left)),
            (lambda: (own.at[1, j, bot], from_m.at[j, bot], right)),
            (lambda: (own.at[3, j, top], from_p.at[j, top], left)),
            (lambda: (own.at[1, j, top], from_m.at[j, top], right)),
            (lambda: (own.at[3, j, bot], from_p.at[j, bot], left)),
        )[k]()
        return remote(src, dst, x_ssem.at[j, k], x_rsem.at[j, k], {"dp": device})

    loads = [
        pltpu.make_async_copy(proj, p_buf, load_sem.at[0]),
        pltpu.make_async_copy(avg, m_buf, load_sem.at[1]),
        pltpu.make_async_copy(avg_sq, v_buf, load_sem.at[2]),
        pltpu.make_async_copy(weight, w_buf, load_sem.at[3]),
    ]

    def start_loads(j):
        for q in (2, 1, 3, 0):
            own_copy(q, j).start()

    def start_sib(j):
        for q in (2, 1, 3, 0):
            sib_copy(q, j).start()

    start_loads(0)
    barrier = pltpu.get_barrier_semaphore()
    for i in range(1, N_DP):
        pl.semaphore_signal(barrier, inc=1, device_id={"dp": (d + i) % N_DP}, device_id_type=MESH)
    for i in range(1, N_FSDP):
        pl.semaphore_signal(barrier, inc=1, device_id={"fsdp": (f + i) % N_FSDP}, device_id_type=MESH)
    pl.semaphore_wait(barrier, N_DP + N_FSDP - 2)

    start_sib(0)
    for copy in loads:
        copy.start()
    for j in range(1, AHEAD):
        start_loads(j)
        start_sib(j)

    loads[0].wait()
    p_bf[...] = p_buf[...].astype(BF16)
    p_t[...] = dot_nt(diagonal((rank, rank), 0, 0).astype(BF16), p_bf[...]).astype(BF16)
    tan_acc[...] = jnp.zeros_like(tan_acc)
    for copy in loads[1:]:
        copy.wait()

    def pair_sum(q, j):
        own_copy(q, j).wait()
        sib_copy(q, j).wait_recv()
        return own[q, j].astype(F32) + sib_in[q, j].astype(F32)

    def stage_pair(j):
        own[2, j] = pair_sum(2, j).astype(BF16)
        x_copy(0, j).start()
        x_copy(1, j).start()
        own[1, j] = pair_sum(1, j).astype(BF16)
        x_copy(2, j).start()
        own[3, j] = pair_sum(3, j).astype(BF16)
        x_copy(3, j).start()

    def stage_pass(j):
        x_copy(0, j).wait_recv()
        own[1, j, top] = (own[1, j, top].astype(F32) + opp_top[j].astype(F32)).astype(BF16)
        x_copy(4, j).start()
        x_copy(1, j).wait_recv()
        own[3, j, bot] = (own[3, j, bot].astype(F32) + opp_bot[j].astype(F32)).astype(BF16)
        x_copy(5, j).start()

    def stage_low(j):
        total = pair_sum(0, j)
        for k in (2, 3, 4, 5):
            x_copy(k, j).wait_recv()
        total = (total + from_m[j].astype(F32) + from_p[j].astype(F32)).astype(BF16)
        own[0, j] = total
        low_part[j] = dot(p_t[...], total).astype(BF16).reshape(N_FSDP, share, CHUNK)

        @pl.loop(1, N_FSDP)
        def _(i):
            to = (f + i) % N_FSDP
            remote(low_part.at[j, to], low_in.at[j, f], low_ssem.at[j], low_rsem.at[j], {"fsdp": to}).start()

    def stage_adam(j):
        others = low_in.at[j, pl.ds(0, N_FSDP - 1)]
        low_in[j, f] = low_part[j, f]
        pltpu.make_async_copy(others, others, low_rsem.at[j]).wait()
        low = jnp.sum(low_in[j].astype(F32), axis=0)
        cols = step_columns(j)
        one = 0.9 * m_buf[:, cols] + 0.1 * low
        two = 0.999 * v_buf[:, cols] + 0.001 * low * low
        m_buf[:, cols] = one
        v_buf[:, cols] = two
        low_norm[j, f, 0] = low.astype(BF16)
        low_norm[j, f, 1] = (one / (jnp.sqrt(two) + 1e-08)).astype(BF16)

        @pl.loop(1, N_FSDP)
        def _(i):
            to = (f + i) % N_FSDP
            remote(low_norm.at[j, f], low_norm.at[j, f], ln_ssem.at[j], ln_rsem.at[j], {"fsdp": to}).start()

    def stage_tangent(j):
        others = low_norm.at[j, pl.ds(0, N_FSDP - 1)]
        pltpu.make_async_copy(others, others, ln_rsem.at[j]).wait()
        low = low_norm[j, :, 0].reshape(rank, CHUNK)
        resid = (own[0, j].astype(F32) - dot(p_bf[...], low)).astype(BF16)
        tan_acc[...] += dot_nt(resid, low)

    def stage_weight(j):
        cols = step_columns(j)
        update = dot(p_bf[...], low_norm[j, :, 1].reshape(rank, CHUNK))
        w_buf[:, cols] = (w_buf[:, cols].astype(F32) - 2.0 * update).astype(BF16)

    @pl.loop(0, steps + 4)
    def _(t):
        @pl.when(t + AHEAD < steps)
        def _():
            start_loads(t + AHEAD)
            start_sib(t + AHEAD)

        @pl.when(t < steps)
        def _():
            stage_pair(t)

        @pl.when((t >= 1) & (t < steps + 1))
        def _():
            stage_pass(t - 1)

        @pl.when((t >= 2) & (t < steps + 2))
        def _():
            stage_low(t - 2)

        @pl.when((t >= 3) & (t < steps + 3))
        def _():
            stage_adam(t - 3)

        @pl.when(t >= 4)
        def _():
            stage_tangent(t - 4)

    tan_send[...] = tan_acc[...].astype(BF16).reshape(N_DP, tan_rows, rank)

    @pl.loop(1, N_DP)
    def _(i):
        to = (d + i) % N_DP
        remote(tan_send.at[to], tan_in.at[d], tail_ssem.at[0], tail_rsem.at[0], {"dp": to}).start()

    tan_in[d] = tan_send[d]

    @pl.loop(0, steps)
    def _(j):
        stage_weight(j)

    outs = [
        pltpu.make_async_copy(w_buf, new_weight, out_sem.at[0]),
        pltpu.make_async_copy(m_buf, moment_one, out_sem.at[1]),
        pltpu.make_async_copy(v_buf, moment_two, out_sem.at[2]),
    ]
    for copy in outs:
        copy.start()

    others = tan_in.at[pl.ds(0, N_DP - 1)]
    pltpu.make_async_copy(others, others, tail_rsem.at[0]).wait()
    tan_all[d] = jnp.sum(tan_in[...].astype(F32), axis=0).astype(BF16)

    @pl.loop(1, N_DP)
    def _(i):
        to = (d + i) % N_DP
        remote(tan_all.at[d], tan_all.at[d], tail_ssem.at[1], tail_rsem.at[1], {"dp": to}).start()

    proj_sq = fold_rows(p_buf[...] * p_buf[...])
    pick = diagonal((tan_rows, rank), d * tan_rows, 0).astype(BF16)
    proj_pick = dot_nt(pick, p_bf[...]).astype(BF16)

    others = tan_all.at[pl.ds(0, N_DP - 1)]
    pltpu.make_async_copy(others, others, tail_rsem.at[1]).wait()

    tan = tan_all[...].reshape(rank, rank)
    tan_pick = dot_nt(pick, tan).astype(BF16)
    picks = jnp.concatenate([proj_pick, tan_pick], axis=0)
    with_proj = dot(picks, p_bf[...])
    with_tan = dot(picks, tan)
    gram_pp = with_proj[:tan_rows]
    gram_pt = with_proj[tan_rows:] + with_tan[:tan_rows]
    gram_tt = with_tan[tan_rows:]
    tan_f = tan.astype(F32)
    stats = jnp.concatenate([fold_rows(tan_f * tan_f), proj_sq], axis=0).astype(BF16)
    for to_y in range(4):
        for to_z in range(4):
            block = (slice(16 * to_y, 16 * to_y + 16), slice(128 * to_z, 128 * to_z + 128))
            at = 4 * to_y + to_z
            gram_send[at, 0:16] = gram_pp[block].astype(BF16)
            gram_send[at, 16:32] = gram_pt[block].astype(BF16)
            gram_send[at, 32:48] = gram_tt[block].astype(BF16)
            gram_send[at, 48:64] = stats

    @pl.loop(1, N_FSDP)
    def _(i):
        to = (f + i) % N_FSDP
        remote(gram_send.at[to], gram_in.at[f], tail_ssem.at[2], tail_rsem.at[2], {"fsdp": to}).start()

    gram_in[f] = gram_send[f]
    others = gram_in.at[pl.ds(0, N_FSDP - 1)]
    pltpu.make_async_copy(others, others, tail_rsem.at[2]).wait()
    sums = jnp.sum(gram_in[...].astype(F32), axis=0)
    tan_total = jnp.sum(sums[48:56])
    proj_total = jnp.sum(sums[56:64])
    tan_scale = 0.5 * jnp.sqrt(F32(rank)) / jnp.sqrt(jnp.full((1, 1), tan_total, F32) + 1e-06)
    middle = (proj_total + tan_scale * tan_scale * tan_total) / rank
    block = sums[0:16] + tan_scale * sums[16:32] + tan_scale * tan_scale * sums[32:48]
    on_diagonal = diagonal((16, 128), d * tan_rows + (f // 4) * 16, (f % 4) * 128)
    gram_all[d, f] = (block - jnp.where(on_diagonal, middle, 0.0)).astype(BF16)

    @pl.loop(1, N_FSDP)
    def _(i):
        to = (f + i) % N_FSDP
        remote(gram_all.at[d, f], gram_all.at[d, f], tail_ssem.at[3], tail_rsem.at[3], {"fsdp": to}).start()

    others = gram_all.at[d, pl.ds(0, N_FSDP - 1)]
    pltpu.make_async_copy(others, others, tail_rsem.at[3]).wait()

    @pl.loop(1, N_DP)
    def _(i):
        to = (d + i) % N_DP
        remote(gram_all.at[d], gram_all.at[d], tail_ssem.at[4], tail_rsem.at[4], {"dp": to}).start()

    frame = p_buf[...] + tan_scale * tan_f
    out_buf[...] = frame
    others = gram_all.at[pl.ds(0, N_DP - 1)]
    pltpu.make_async_copy(others, others, tail_rsem.at[4]).wait()

    eye = diagonal((rank, rank), 0, 0)
    whole = gram_all[...].astype(F32).reshape(N_DP, 4, 4, 16, 128)
    gram = jnp.concatenate([whole[:, :, at].reshape(rank, 128) for at in range(4)], axis=1)
    gram = gram + jnp.where(eye, middle, 0.0)
    frame_sq = jnp.sum(jnp.where(eye, gram, 0.0))
    frame_sq = jnp.full((1, 1), frame_sq, F32) + 1e-06
    gram_buf[...] = gram * (1.0 / frame_sq)
    q_buf[...] = jnp.where(eye, 1.0, 0.0)

    def polynomial(gram_parts):
        squared = dot3(gram_parts, gram_parts)
        return COEF_B * gram_buf[...] + COEF_C * squared + jnp.where(diagonal((rank, rank), 0, 0), COEF_A, 0.0)

    @pl.loop(0, NS_ITERS - 1)
    def _(sweep):
        gram_parts = split(gram_buf[...])
        poly = split(polynomial(gram_parts))
        once = dot3(gram_parts, poly)
        q_buf[...] = dot3(split(q_buf[...]), poly)
        gram_buf[...] = dot3(split(once), poly)

    poly = split(polynomial(split(gram_buf[...])))
    q_all = dot3(split(q_buf[...]), poly) * (1.0 / jnp.sqrt(frame_sq))
    out_buf[...] = dot3(split(out_buf[...]), split(q_all))
    last = pltpu.make_async_copy(out_buf, new_proj, out_sem.at[3])
    last.start()

    @pl.loop(0, steps)
    def _(j):
        for q in range(N_X):
            sib_copy(q, j).wait_send()
        for k in range(6):
            x_copy(k, j).wait_send()
        others = low_in.at[j, pl.ds(0, N_FSDP - 1)]
        pltpu.make_async_copy(others, others, low_ssem.at[j]).wait()
        others = low_norm.at[j, pl.ds(0, N_FSDP - 1)]
        pltpu.make_async_copy(others, others, ln_ssem.at[j]).wait()

    for k, others in enumerate(
        (
            tan_in.at[pl.ds(0, N_DP - 1)],
            tan_all.at[pl.ds(0, N_DP - 1)],
            gram_in.at[pl.ds(0, N_FSDP - 1)],
            gram_all.at[0, pl.ds(0, N_FSDP - 1)],
            gram_all.at[pl.ds(0, N_DP - 1)],
        )
    ):
        pltpu.make_async_copy(others, others, tail_ssem.at[k]).wait()
    for copy in outs:
        copy.wait()
    last.wait()


def on_device(grad_parts, weight, projector, exp_avg, exp_avg_sq):
    grad = grad_parts.reshape(grad_parts.shape[1:])
    rows = grad.shape[0]
    rank = projector.shape[1]
    share, owned = exp_avg.shape
    steps = owned // CHUNK
    tan_rows = rank // N_DP
    vmem = pltpu.VMEM
    dma = pltpu.SemaphoreType.DMA
    hbm = pl.BlockSpec(memory_space=pl.ANY)
    return pl.pallas_call(
        kernel,
        out_shape=(
            jax.ShapeDtypeStruct(weight.shape, weight.dtype),
            jax.ShapeDtypeStruct(projector.shape, projector.dtype),
            jax.ShapeDtypeStruct(exp_avg.shape, exp_avg.dtype),
            jax.ShapeDtypeStruct(exp_avg_sq.shape, exp_avg_sq.dtype),
        ),
        in_specs=[hbm] * 5,
        out_specs=(hbm,) * 4,
        scratch_shapes=[
            vmem((N_X, steps, rows, CHUNK), BF16),
            vmem((N_X, steps, rows, CHUNK), BF16),
            vmem((steps, rows // 2, CHUNK), BF16),
            vmem((steps, rows // 2, CHUNK), BF16),
            vmem((steps, rows, CHUNK), BF16),
            vmem((steps, rows, CHUNK), BF16),
            vmem((steps, N_FSDP, share, CHUNK), BF16),
            vmem((steps, N_FSDP, share, CHUNK), BF16),
            vmem((steps, N_FSDP, 2, share, CHUNK), BF16),
            vmem(weight.shape, BF16),
            vmem(projector.shape, F32),
            vmem(exp_avg.shape, F32),
            vmem(exp_avg_sq.shape, F32),
            vmem(projector.shape, BF16),
            vmem((rank, rows), BF16),
            vmem((rows, rank), F32),
            vmem((N_DP, tan_rows, rank), BF16),
            vmem((N_DP, tan_rows, rank), BF16),
            vmem((N_DP, tan_rows, rank), BF16),
            vmem((N_FSDP, 64, 128), BF16),
            vmem((N_FSDP, 64, 128), BF16),
            vmem((N_DP, N_FSDP, 16, 128), BF16),
            vmem((rank, rank), F32),
            vmem((rank, rank), F32),
            vmem((rows, rank), F32),
            dma((4,)),
            dma((steps, N_X)),
            dma((steps, N_X)),
            dma((steps, N_X)),
            dma((steps, 6)),
            dma((steps, 6)),
            dma((steps,)),
            dma((steps,)),
            dma((steps,)),
            dma((steps,)),
            dma((5,)),
            dma((5,)),
            dma((4,)),
        ],
        compiler_params=pltpu.CompilerParams(
            collective_id=0, has_side_effects=True, vmem_limit_bytes=60 * 1024 * 1024
        ),
    )(grad, weight, projector, exp_avg, exp_avg_sq)


def solution(mesh):
    return jax.shard_map(
        on_device,
        mesh=mesh,
        in_specs=(
            P("dp", "fsdp", None),
            P("fsdp", "dp"),
            P("fsdp", None),
            P("fsdp", "dp"),
            P("fsdp", "dp"),
        ),
        out_specs=(P("fsdp", "dp"), P("fsdp", None), P("fsdp", "dp"), P("fsdp", "dp")),
        check_vma=False,
    )
```

```python
import jax
import jax.numpy as jnp
from jax import lax
from jax.experimental import pallas as pl
from jax.experimental.pallas import tpu as pltpu
from jax.sharding import PartitionSpec as P

NS_ITERS = 5

COEF_A = 3.4445
COEF_B = -4.775
COEF_C = 2.0315

MESH = pl.DeviceIdType.MESH
BF16 = jnp.bfloat16
F32 = jnp.float32

N_X = 4
N_DP = 8
N_FSDP = 16
N_CHIPS = N_X * N_FSDP
WIDTHS = (256,) * 7
AHEAD = 2
NORM_EARLY = 3


def dot(left, right):
    return jnp.dot(left, right, preferred_element_type=F32)


def dot_nt(left, right):
    return lax.dot_general(left, right, (((1,), (1,)), ((), ())), preferred_element_type=F32)


def diagonal(shape, row_at, col_at):
    rows = lax.broadcasted_iota(jnp.int32, shape, 0) + row_at
    cols = lax.broadcasted_iota(jnp.int32, shape, 1) + col_at
    return rows == cols


def fold_rows(value):
    rows, cols = value.shape
    part = jnp.sum(value.reshape(rows // 8, 8, cols), axis=0)
    total = part[:, 0:128]
    for at in range(128, cols, 128):
        total = total + part[:, at : at + 128]
    return total


def kernel(
    grad, weight, proj, avg, avg_sq,
    new_weight, moment_one, moment_two, tan_out, gram_out, scale_out,
    own, sib_in, opp_top, opp_bot, from_m, from_p,
    low_part, low_in, low_all, norm_all,
    w_buf, p_buf, m_buf, v_buf, p_bf, p_t, tan_acc,
    tan_send, tan_sib, tan_x, tan_in, tan_all, gram_send, gram_in, gram_all, scale_buf,
    load_sem, own_sem, sib_ssem, sib_rsem, x_ssem, x_rsem,
    low_ssem, low_rsem, all_ssem, all_rsem, norm_ssem, norm_rsem, tail_ssem, tail_rsem, out_sem,
):
    rows = grad.shape[0]
    rank = proj.shape[1]
    owned = avg.shape[1]
    steps = len(WIDTHS)
    half = rows // 2
    tan_rows = rank // N_DP

    d = lax.axis_index("dp")
    f = lax.axis_index("fsdp")
    x = d // 2
    core = d % 2
    sib = {"dp": 2 * x + (1 - core)}
    right = {"dp": 2 * ((x + 1) % N_X) + core}
    left = {"dp": 2 * ((x + 3) % N_X) + core}

    def remote(src, dst, ssem, rsem, device):
        return pltpu.make_async_remote_copy(
            src_ref=src, dst_ref=dst, send_sem=ssem, recv_sem=rsem, device_id=device, device_id_type=MESH
        )

    def wait_bytes(ref, sem):
        pltpu.make_async_copy(ref, ref, sem).wait()

    def to_fsdp(src_of, dst, ssem, rsem):
        @pl.loop(1, N_FSDP)
        def _(i):
            to = (f + i) % N_FSDP
            remote(src_of(to), dst, ssem, rsem, {"fsdp": to}).start()

    def to_x(src_of, dst, ssem, rsem):
        for i in (2, 1, 3):
            to = (x + i) % N_X
            remote(src_of(to), dst, ssem, rsem, {"dp": 2 * to + core}).start()

    def chip_at(i):
        to = (x * N_FSDP + f + i) % N_CHIPS
        return {"dp": 2 * (to // N_FSDP) + core, "fsdp": to % N_FSDP}

    starts = [sum(WIDTHS[:j]) for j in range(steps)]
    cols = [pl.ds(starts[j], WIDTHS[j]) for j in range(steps)]

    def columns(owner, j):
        return pl.ds(pl.multiple_of(owner * owned + starts[j], 128), WIDTHS[j])

    def own_copy(q, j):
        return pltpu.make_async_copy(
            grad.at[:, columns(2 * ((x + q) % N_X) + core, j)], own.at[q, :, cols[j]], own_sem.at[j, q]
        )

    def sib_copy(q, j):
        return remote(
            grad.at[:, columns(2 * ((x + q) % N_X) + (1 - core), j)],
            sib_in.at[q, :, cols[j]], sib_ssem.at[j, q], sib_rsem.at[j, q], sib,
        )

    top, bot = pl.ds(0, half), pl.ds(half, half)

    def x_copy(k, j):
        c = cols[j]
        src, dst, device = (
            (own.at[2, top, c], opp_top.at[:, c], right),
            (own.at[2, bot, c], opp_bot.at[:, c], left),
            (own.at[1, bot, c], from_m.at[bot, c], right),
            (own.at[3, top, c], from_p.at[top, c], left),
            (own.at[1, top, c], from_m.at[top, c], right),
            (own.at[3, bot, c], from_p.at[bot, c], left),
        )[k]
        return remote(src, dst, x_ssem.at[j, k], x_rsem.at[j, k], device)

    loads = [
        pltpu.make_async_copy(proj, p_buf, load_sem.at[0]),
        pltpu.make_async_copy(avg, m_buf, load_sem.at[1]),
        pltpu.make_async_copy(avg_sq, v_buf, load_sem.at[2]),
        pltpu.make_async_copy(weight, w_buf, load_sem.at[3]),
    ]

    def start_loads(j):
        for q in (2, 1, 3, 0):
            own_copy(q, j).start()

    def start_sib(j):
        for q in (2, 1, 3, 0):
            sib_copy(q, j).start()

    loads[0].start()
    start_loads(0)
    barrier = pltpu.get_barrier_semaphore()
    pl.semaphore_signal(barrier, inc=1, device_id=sib, device_id_type=MESH)
    for i in range(1, N_CHIPS):
        pl.semaphore_signal(barrier, inc=1, device_id=chip_at(i), device_id_type=MESH)
    loads[0].wait()
    p_bf[...] = p_buf[...].astype(BF16)
    p_t[...] = dot_nt(diagonal((rank, rank), 0, 0).astype(BF16), p_bf[...]).astype(BF16)
    pl.semaphore_wait(barrier, N_CHIPS)

    def pair_sum(q, j):
        own_copy(q, j).wait()
        sib_copy(q, j).wait_recv()
        return own[q, :, cols[j]].astype(F32) + sib_in[q, :, cols[j]].astype(F32)

    def stage_pair(j):
        own[2, :, cols[j]] = pair_sum(2, j).astype(BF16)
        x_copy(0, j).start()
        x_copy(1, j).start()
        own[1, :, cols[j]] = pair_sum(1, j).astype(BF16)
        x_copy(2, j).start()
        own[3, :, cols[j]] = pair_sum(3, j).astype(BF16)
        x_copy(3, j).start()

    def stage_pass(j):
        c = cols[j]
        x_copy(0, j).wait_recv()
        own[1, top, c] = (own[1, top, c].astype(F32) + opp_top[:, c].astype(F32)).astype(BF16)
        x_copy(4, j).start()
        x_copy(1, j).wait_recv()
        own[3, bot, c] = (own[3, bot, c].astype(F32) + opp_bot[:, c].astype(F32)).astype(BF16)
        x_copy(5, j).start()

    def stage_low(j):
        c = cols[j]
        total = pair_sum(0, j)
        for k in (2, 3, 4, 5):
            x_copy(k, j).wait_recv()
        total = (total + from_m[:, c].astype(F32) + from_p[:, c].astype(F32)).astype(BF16)
        own[0, :, c] = total
        low_part[:, :, c] = dot(p_t[...], total).astype(BF16).reshape(N_FSDP, -1, WIDTHS[j])
        to_fsdp(lambda to: low_part.at[to, :, c], low_in.at[f, :, c], low_ssem.at[j], low_rsem.at[j])

    def stage_adam(j):
        c = cols[j]
        low_in[f, :, c] = low_part[f, :, c]
        wait_bytes(low_in.at[pl.ds(0, N_FSDP - 1), :, c], low_rsem.at[j])
        low = jnp.sum(low_in[:, :, c].astype(F32), axis=0)
        low_all[f, :, c] = low.astype(BF16)
        to_fsdp(lambda to: low_all.at[f, :, c], low_all.at[f, :, c], all_ssem.at[j], all_rsem.at[j])
        one = 0.9 * m_buf[:, c] + 0.1 * low
        two = 0.999 * v_buf[:, c] + 0.001 * low * low
        m_buf[:, c] = one
        v_buf[:, c] = two
        norm_all[f, :, c] = (one / (jnp.sqrt(two) + 1e-08)).astype(BF16)

    def stage_norm(j):
        c = cols[j]
        to_fsdp(lambda to: norm_all.at[f, :, c], norm_all.at[f, :, c], norm_ssem.at[j], norm_rsem.at[j])

    def stage_tangent(j):
        c = cols[j]
        wait_bytes(low_all.at[pl.ds(0, N_FSDP - 1), :, c], all_rsem.at[j])
        low = low_all[:, :, c].reshape(rank, WIDTHS[j])
        resid = (own[0, :, c].astype(F32) - dot(p_bf[...], low)).astype(BF16)
        if j == 0:
            tan_acc[...] = dot_nt(resid, low)
        else:
            tan_acc[...] += dot_nt(resid, low)

    def weight_copy(j):
        return pltpu.make_async_copy(w_buf.at[:, cols[j]], new_weight.at[:, cols[j]], out_sem.at[j])

    def stage_weight(j):
        c = cols[j]
        wait_bytes(norm_all.at[pl.ds(0, N_FSDP - 1), :, c], norm_rsem.at[j])
        update = dot(p_bf[...], norm_all[:, :, c].reshape(rank, WIDTHS[j]))
        w_buf[:, c] = (w_buf[:, c].astype(F32) - 2.0 * update).astype(BF16)
        weight_copy(j).start()

    start_sib(0)
    for j in range(1, AHEAD):
        start_loads(j)
        start_sib(j)
    for copy in loads[1:]:
        copy.start()

    for t in range(steps + 4):
        if t + AHEAD < steps:
            start_loads(t + AHEAD)
            start_sib(t + AHEAD)
        if t < steps:
            stage_pair(t)
        if t == 1:
            for copy in loads[1:]:
                copy.wait()
        if 1 <= t < steps + 1:
            stage_pass(t - 1)
        if 2 <= t < steps + 2:
            stage_low(t - 2)
        if 3 <= t < steps + 3:
            stage_adam(t - 3)
        if 4 <= t:
            stage_tangent(t - 4)
            if t - 4 < NORM_EARLY:
                stage_norm(t - 4)
        if 6 <= t < NORM_EARLY + 6:
            stage_weight(t - 6)

    tan_send[...] = tan_acc[...].astype(BF16).reshape(N_X, 2, tan_rows, rank)
    pair_copy = remote(tan_send.at[:, 1 - core], tan_sib, tail_ssem.at[0], tail_rsem.at[0], sib)
    pair_copy.start()
    pair_copy.wait_recv()
    tan_x[...] = (tan_send[:, core].astype(F32) + tan_sib[...].astype(F32)).astype(BF16)
    to_x(lambda to: tan_x.at[to], tan_in.at[x], tail_ssem.at[1], tail_rsem.at[1])
    tan_in[x] = tan_x[x]
    for j in range(NORM_EARLY, steps):
        stage_norm(j)
    outs = [
        pltpu.make_async_copy(m_buf, moment_one, out_sem.at[steps]),
        pltpu.make_async_copy(v_buf, moment_two, out_sem.at[steps + 1]),
    ]
    for copy in outs:
        copy.start()
    wait_bytes(tan_in.at[pl.ds(0, N_X - 1)], tail_rsem.at[1])
    tan_all[x, core] = jnp.sum(tan_in[...].astype(F32), axis=0).astype(BF16)
    to_x(lambda to: tan_all.at[x, core], tan_all.at[x, core], tail_ssem.at[2], tail_rsem.at[2])

    for j in range(NORM_EARLY, NORM_EARLY + 2):
        stage_weight(j)
    proj_sq = fold_rows(p_buf[...] * p_buf[...])
    pick = diagonal((tan_rows, rank), d * tan_rows, 0).astype(BF16)
    proj_pick = dot_nt(pick, p_bf[...]).astype(BF16)

    wait_bytes(tan_all.at[pl.ds(0, N_X - 1), 0], tail_rsem.at[2])
    pair_all = remote(tan_all.at[:, core], tan_all.at[:, core], tail_ssem.at[3], tail_rsem.at[3], sib)
    pair_all.start()
    pair_all.wait_recv()

    tan = tan_all[...].reshape(rank, rank)
    tan_copy = pltpu.make_async_copy(tan_all, tan_out, out_sem.at[steps + 2])
    tan_copy.start()
    tan_pick = dot_nt(pick, tan).astype(BF16)
    picks = jnp.concatenate([proj_pick, tan_pick], axis=0)
    with_proj = dot(picks, p_bf[...])
    with_tan = dot(picks, tan)
    gram_pp = with_proj[:tan_rows]
    gram_pt = with_proj[tan_rows:] + with_tan[:tan_rows]
    gram_tt = with_tan[tan_rows:]
    tan_f = tan.astype(F32)
    stats = jnp.concatenate([fold_rows(tan_f * tan_f), proj_sq], axis=0).astype(BF16)
    for to_y in range(4):
        for to_z in range(4):
            block = (slice(16 * to_y, 16 * to_y + 16), slice(128 * to_z, 128 * to_z + 128))
            at = 4 * to_y + to_z
            gram_send[at, 0:16] = gram_pp[block].astype(BF16)
            gram_send[at, 16:32] = gram_pt[block].astype(BF16)
            gram_send[at, 32:48] = gram_tt[block].astype(BF16)
            gram_send[at, 48:64] = stats
    to_fsdp(lambda to: gram_send.at[to], gram_in.at[f], tail_ssem.at[4], tail_rsem.at[4])
    gram_in[f] = gram_send[f]
    for j in range(NORM_EARLY + 2, steps):
        stage_weight(j)
    wait_bytes(gram_in.at[pl.ds(0, N_FSDP - 1)], tail_rsem.at[4])
    sums = jnp.sum(gram_in[...].astype(F32), axis=0)
    tan_total = jnp.sum(sums[48:56])
    proj_total = jnp.sum(sums[56:64])
    tan_scale = 0.5 * jnp.sqrt(F32(rank)) / jnp.sqrt(jnp.full((1, 1), tan_total, F32) + 1e-06)
    middle = (proj_total + tan_scale * tan_scale * tan_total) / rank
    block = sums[0:16] + tan_scale * sums[16:32] + tan_scale * tan_scale * sums[32:48]
    on_diagonal = diagonal((16, 128), d * tan_rows + (f // 4) * 16, (f % 4) * 128)
    gram_all[x, core, f] = (block - jnp.where(on_diagonal, middle, 0.0)).astype(BF16)
    mine = gram_all.at[x, core, f]

    @pl.loop(1, N_CHIPS)
    def _(i):
        remote(mine, mine, tail_ssem.at[5], tail_rsem.at[5], chip_at(i)).start()

    scale_buf[0:8] = jnp.broadcast_to(tan_scale, (8, 128))
    scale_buf[8:16] = jnp.broadcast_to(middle, (8, 128))
    scale_copy = pltpu.make_async_copy(scale_buf, scale_out, out_sem.at[steps + 3])
    scale_copy.start()
    blocks = own.at[0, pl.ds(0, 144), pl.ds(0, 896)]
    wait_bytes(blocks, tail_rsem.at[5])
    pair_gram = remote(gram_all.at[:, core], gram_all.at[:, core], tail_ssem.at[7], tail_rsem.at[7], sib)
    pair_gram.start()
    pair_gram.wait_recv()
    gram_copy = pltpu.make_async_copy(gram_all, gram_out, out_sem.at[steps + 4])
    gram_copy.start()

    for j in range(steps):
        c = cols[j]
        for q in range(N_X):
            sib_copy(q, j).wait_send()
        for k in range(6):
            x_copy(k, j).wait_send()
        wait_bytes(low_in.at[pl.ds(0, N_FSDP - 1), :, c], low_ssem.at[j])
        wait_bytes(low_all.at[pl.ds(0, N_FSDP - 1), :, c], all_ssem.at[j])
        wait_bytes(norm_all.at[pl.ds(0, N_FSDP - 1), :, c], norm_ssem.at[j])
        weight_copy(j).wait()
    pair_copy.wait_send()
    wait_bytes(tan_in.at[pl.ds(0, N_X - 1)], tail_ssem.at[1])
    wait_bytes(tan_all.at[pl.ds(0, N_X - 1), 0], tail_ssem.at[2])
    pair_all.wait_send()
    wait_bytes(gram_in.at[pl.ds(0, N_FSDP - 1)], tail_ssem.at[4])
    wait_bytes(blocks, tail_ssem.at[5])
    pair_gram.wait_send()
    for copy in outs:
        copy.wait()
    tan_copy.wait()
    scale_copy.wait()
    gram_copy.wait()


def finish_kernel(
    weight_in, one_in, two_in, tan, gram, scale, proj,
    new_weight, new_proj, moment_one, moment_two,
    tan_buf, gram_buf, scale_buf, proj_buf, w_state, q_state, out_buf, weight_buf, one_buf, two_buf, sems,
):
    rank = proj.shape[1]
    copies = [
        pltpu.make_async_copy(gram, gram_buf, sems.at[0]),
        pltpu.make_async_copy(scale, scale_buf, sems.at[1]),
        pltpu.make_async_copy(tan, tan_buf, sems.at[2]),
        pltpu.make_async_copy(proj, proj_buf, sems.at[3]),
        pltpu.make_async_copy(weight_in, weight_buf, sems.at[4]),
        pltpu.make_async_copy(one_in, one_buf, sems.at[5]),
        pltpu.make_async_copy(two_in, two_buf, sems.at[6]),
    ]
    passed = [
        pltpu.make_async_copy(weight_buf, new_weight, sems.at[4]),
        pltpu.make_async_copy(one_buf, moment_one, sems.at[5]),
        pltpu.make_async_copy(two_buf, moment_two, sems.at[6]),
    ]
    for copy in copies:
        copy.start()
    copies[0].wait()
    copies[1].wait()
    tan_scale = scale_buf[0:1, 0:1]
    middle = scale_buf[8:9, 0:1]
    eye = diagonal((rank, rank), 0, 0)
    whole = gram_buf[...].astype(F32).reshape(N_DP, 4, 4, 16, 128)
    gram_dev = jnp.concatenate([whole[:, :, at].reshape(rank, 128) for at in range(4)], axis=1)
    trace_dev = jnp.sum(jnp.sum(jnp.where(eye, gram_dev, 0.0), axis=0, keepdims=True), axis=1, keepdims=True)
    frame_sq = trace_dev + rank * middle + 1e-06
    inverse = 1.0 / frame_sq
    shift = trace_dev / rank
    center = (middle + shift) * inverse
    state = (gram_dev - jnp.where(eye, shift, 0.0)) * inverse
    w_state[...] = state
    q_center = None
    for sweep in range(NS_ITERS):
        state = w_state[...]
        state_b = state.astype(BF16)
        poly = (COEF_B + 2.0 * COEF_C * center) * state + COEF_C * dot(state_b, state_b)
        poly_center = COEF_A + COEF_B * center + COEF_C * center * center
        poly_b = poly.astype(BF16)
        if sweep == 0:
            q_state[...] = poly
            q_center = poly_center
        else:
            q_now = q_state[...]
            q_state[...] = q_center * poly + poly_center * q_now + dot(q_now.astype(BF16), poly_b)
            q_center = q_center * poly_center
        if sweep == 0:
            for copy, on in zip(copies[4:], passed):
                copy.wait()
                on.start()
        if sweep < NS_ITERS - 1:
            once = center * poly + poly_center * state + dot(state_b, poly_b)
            once_center = center * poly_center
            w_state[...] = once_center * poly + poly_center * once + dot(once.astype(BF16), poly_b)
            center = once_center * poly_center
    q_now = q_state[...]
    q_shift = jnp.sum(jnp.sum(jnp.where(eye, q_now, 0.0), axis=0, keepdims=True), axis=1, keepdims=True) / rank
    q_b = (q_now - jnp.where(eye, q_shift, 0.0)).astype(BF16)
    copies[2].wait()
    copies[3].wait()
    scale_down = 1.0 / jnp.sqrt(frame_sq)
    frame = (proj_buf[...] + tan_scale * tan_buf[...].reshape(rank, rank).astype(F32)) * scale_down
    out_buf[...] = (q_center + q_shift) * frame + dot(frame.astype(BF16), q_b)
    last = pltpu.make_async_copy(out_buf, new_proj, sems.at[7])
    last.start()
    for copy in passed:
        copy.wait()
    last.wait()


def on_device(grad_parts, weight, projector, exp_avg, exp_avg_sq):
    grad = grad_parts.reshape(grad_parts.shape[1:])
    rows = grad.shape[0]
    rank = projector.shape[1]
    share, owned = exp_avg.shape
    steps = len(WIDTHS)
    tan_rows = rank // N_DP
    vmem = pltpu.VMEM
    dma = pltpu.SemaphoreType.DMA
    hbm = pl.BlockSpec(memory_space=pl.ANY)
    shape = jax.ShapeDtypeStruct
    tan_shape = (N_X, 2, tan_rows, rank)
    gram_shape = (N_X, 2, N_FSDP, 16, 128)
    mid = pl.pallas_call(
        kernel,
        out_shape=(
            shape(weight.shape, weight.dtype),
            shape(exp_avg.shape, F32),
            shape(exp_avg_sq.shape, F32),
            shape(tan_shape, BF16),
            shape(gram_shape, BF16),
            shape((16, 128), F32),
        ),
        in_specs=[hbm] * 5,
        out_specs=(hbm,) * 6,
        scratch_shapes=[
            vmem((N_X, rows, owned), BF16),
            vmem((N_X, rows, owned), BF16),
            vmem((rows // 2, owned), BF16),
            vmem((rows // 2, owned), BF16),
            vmem((rows, owned), BF16),
            vmem((rows, owned), BF16),
            vmem((N_FSDP, share, owned), BF16),
            vmem((N_FSDP, share, owned), BF16),
            vmem((N_FSDP, share, owned), BF16),
            vmem((N_FSDP, share, owned), BF16),
            vmem(weight.shape, BF16),
            vmem(projector.shape, F32),
            vmem(exp_avg.shape, F32),
            vmem(exp_avg_sq.shape, F32),
            vmem(projector.shape, BF16),
            vmem((rank, rows), BF16),
            vmem((rows, rank), F32),
            vmem(tan_shape, BF16),
            vmem((N_X, tan_rows, rank), BF16),
            vmem((N_X, tan_rows, rank), BF16),
            vmem((N_X, tan_rows, rank), BF16),
            vmem(tan_shape, BF16),
            vmem((N_FSDP, 64, 128), BF16),
            vmem((N_FSDP, 64, 128), BF16),
            vmem(gram_shape, BF16),
            vmem((16, 128), F32),
            dma((4,)),
            dma((steps, N_X)),
            dma((steps, N_X)),
            dma((steps, N_X)),
            dma((steps, 6)),
            dma((steps, 6)),
            dma((steps,)),
            dma((steps,)),
            dma((steps,)),
            dma((steps,)),
            dma((steps,)),
            dma((steps,)),
            dma((8,)),
            dma((8,)),
            dma((steps + 5,)),
        ],
        compiler_params=pltpu.CompilerParams(
            collective_id=0, has_side_effects=True, vmem_limit_bytes=60 * 1024 * 1024
        ),
    )(grad, weight, projector, exp_avg, exp_avg_sq)
    return pl.pallas_call(
        finish_kernel,
        out_shape=(
            shape(weight.shape, weight.dtype),
            shape(projector.shape, F32),
            shape(exp_avg.shape, F32),
            shape(exp_avg_sq.shape, F32),
        ),
        in_specs=[hbm] * 7,
        out_specs=(hbm,) * 4,
        scratch_shapes=[
            vmem(tan_shape, BF16),
            vmem(gram_shape, BF16),
            vmem((16, 128), F32),
            vmem(projector.shape, F32),
            vmem((rank, rank), F32),
            vmem((rank, rank), F32),
            vmem(projector.shape, F32),
            vmem(weight.shape, BF16),
            vmem(exp_avg.shape, F32),
            vmem(exp_avg_sq.shape, F32),
            dma((8,)),
        ],
        compiler_params=pltpu.CompilerParams(vmem_limit_bytes=60 * 1024 * 1024),
    )(*mid, projector)


def solution(mesh):
    return jax.shard_map(
        on_device,
        mesh=mesh,
        in_specs=(
            P("dp", "fsdp", None),
            P("fsdp", "dp"),
            P("fsdp", None),
            P("fsdp", "dp"),
            P("fsdp", "dp"),
        ),
        out_specs=(P("fsdp", "dp"), P("fsdp", None), P("fsdp", "dp"), P("fsdp", "dp")),
        check_vma=False,
    )
```

```python
import jax
import jax.numpy as jnp
from jax import lax
from jax.experimental import pallas as pl
from jax.experimental.pallas import tpu as pltpu
from jax.sharding import PartitionSpec as P

NS_ITERS = 5

COEF_A = 3.4445
COEF_B = -4.775
COEF_C = 2.0315

MESH = pl.DeviceIdType.MESH
BF16 = jnp.bfloat16
F32 = jnp.float32

N_X = 4
N_DP = 8
N_FSDP = 16
N_CHIPS = N_X * N_FSDP
WIDTHS = (256,) * 7
AHEAD = 2
NORM_EARLY = 3


def dot(left, right):
    return jnp.dot(left, right, preferred_element_type=F32)


def dot_nt(left, right):
    return lax.dot_general(left, right, (((1,), (1,)), ((), ())), preferred_element_type=F32)


def diagonal(shape, row_at, col_at):
    rows = lax.broadcasted_iota(jnp.int32, shape, 0) + row_at
    cols = lax.broadcasted_iota(jnp.int32, shape, 1) + col_at
    return rows == cols


def fold_rows(value):
    rows, cols = value.shape
    part = jnp.sum(value.reshape(rows // 8, 8, cols), axis=0)
    total = part[:, 0:128]
    for at in range(128, cols, 128):
        total = total + part[:, at : at + 128]
    return total


def kernel(
    grad, weight, proj, avg, avg_sq,
    new_weight, moment_one, moment_two, tan_out, gram_out, scale_out,
    own, sib_in, opp_top, opp_bot, from_m, from_p,
    low_part, low_in, low_all, norm_all,
    w_buf, p_buf, m_buf, v_buf, p_bf, p_t, tan_acc,
    tan_send, tan_sib, tan_x, tan_in, tan_all, gram_send, gram_in, gram_all, scale_buf,
    load_sem, own_sem, sib_ssem, sib_rsem, x_ssem, x_rsem,
    low_ssem, low_rsem, all_ssem, all_rsem, norm_ssem, norm_rsem, tail_ssem, tail_rsem, out_sem,
):
    rows = grad.shape[0]
    rank = proj.shape[1]
    owned = avg.shape[1]
    steps = len(WIDTHS)
    half = rows // 2
    tan_rows = rank // N_DP

    d = lax.axis_index("dp")
    f = lax.axis_index("fsdp")
    x, core = lax.div(d, 2), lax.rem(d, 2)
    y, z = lax.div(f, 4), lax.rem(f, 4)
    xs = [lax.rem(x + i, N_X) for i in range(N_X)]
    ys = [lax.rem(y + i, 4) for i in range(4)]
    zs = [lax.rem(z + i, 4) for i in range(4)]
    far = (2, 1, 3, 0)
    hops = (0, 1, 2, 1)
    sib = {"dp": 2 * x + (1 - core)}
    right = {"dp": 2 * xs[1] + core}
    left = {"dp": 2 * xs[3] + core}

    def remote(src, dst, ssem, rsem, device):
        return pltpu.make_async_remote_copy(
            src_ref=src, dst_ref=dst, send_sem=ssem, recv_sem=rsem, device_id=device, device_id_type=MESH
        )

    def wait_bytes(ref, sem):
        pltpu.make_async_copy(ref, ref, sem).wait()

    planes = sorted(((i, j) for i in range(4) for j in range(4)), key=lambda at: -hops[at[0]] - hops[at[1]])[:-1]
    chips = sorted(
        ((k, i, j) for k in range(4) for i in range(4) for j in range(4)),
        key=lambda at: -hops[at[0]] - hops[at[1]] - hops[at[2]],
    )[:-1]

    def to_fsdp(src_of, dst, ssem, rsem, ordered=False):
        if ordered:
            for i, j in planes:
                to = 4 * ys[i] + zs[j]
                remote(src_of(to), dst, ssem, rsem, {"fsdp": to}).start()
            return

        @pl.loop(1, N_FSDP)
        def _(i):
            to = lax.rem(f + i, N_FSDP)
            remote(src_of(to), dst, ssem, rsem, {"fsdp": to}).start()

    def to_x(src_of, dst, ssem, rsem):
        for i in far[:3]:
            to = xs[i]
            remote(src_of(to), dst, ssem, rsem, {"dp": 2 * to + core}).start()

    def chip_at(at):
        return {"dp": 2 * xs[at[0]] + core, "fsdp": 4 * ys[at[1]] + zs[at[2]]}

    starts = [sum(WIDTHS[:j]) for j in range(steps)]
    cols = [pl.ds(starts[j], WIDTHS[j]) for j in range(steps)]

    def columns(owner, j):
        return pl.ds(pl.multiple_of(owner * owned + starts[j], 128), WIDTHS[j])

    def own_copy(q, j):
        return pltpu.make_async_copy(
            grad.at[:, columns(2 * xs[q] + core, j)], own.at[q, :, cols[j]], own_sem.at[j, q]
        )

    def sib_copy(q, j):
        return remote(
            grad.at[:, columns(2 * xs[q] + (1 - core), j)],
            sib_in.at[q, :, cols[j]], sib_ssem.at[j, q], sib_rsem.at[j, q], sib,
        )

    top, bot = pl.ds(0, half), pl.ds(half, half)

    def x_copy(k, j):
        c = cols[j]
        src, dst, device = (
            (own.at[2, top, c], opp_top.at[:, c], right),
            (own.at[2, bot, c], opp_bot.at[:, c], left),
            (own.at[1, bot, c], from_m.at[bot, c], right),
            (own.at[3, top, c], from_p.at[top, c], left),
            (own.at[1, top, c], from_m.at[top, c], right),
            (own.at[3, bot, c], from_p.at[bot, c], left),
        )[k]
        return remote(src, dst, x_ssem.at[j, k], x_rsem.at[j, k], device)

    loads = [
        pltpu.make_async_copy(proj, p_buf, load_sem.at[0]),
        pltpu.make_async_copy(avg, m_buf, load_sem.at[1]),
        pltpu.make_async_copy(avg_sq, v_buf, load_sem.at[2]),
        pltpu.make_async_copy(weight, w_buf, load_sem.at[3]),
    ]

    def start_loads(j):
        for q in (2, 1, 3, 0):
            own_copy(q, j).start()

    def start_sib(j):
        for q in (2, 1, 3, 0):
            sib_copy(q, j).start()

    loads[0].start()
    start_loads(0)
    barrier = pltpu.get_barrier_semaphore()
    pl.semaphore_signal(barrier, inc=1, device_id=sib, device_id_type=MESH)
    for i in range(1, N_CHIPS):
        to = lax.rem(x * N_FSDP + f + i, N_CHIPS)
        device = {"dp": 2 * lax.div(to, N_FSDP) + core, "fsdp": lax.rem(to, N_FSDP)}
        pl.semaphore_signal(barrier, inc=1, device_id=device, device_id_type=MESH)
    pl.semaphore_wait(barrier, N_CHIPS)

    def pair_sum(q, j):
        own_copy(q, j).wait()
        sib_copy(q, j).wait_recv()
        return own[q, :, cols[j]].astype(F32) + sib_in[q, :, cols[j]].astype(F32)

    def stage_opposite(j):
        own[2, :, cols[j]] = pair_sum(2, j).astype(BF16)
        x_copy(0, j).start()
        x_copy(1, j).start()

    def stage_pair(j):
        own[1, :, cols[j]] = pair_sum(1, j).astype(BF16)
        x_copy(2, j).start()
        own[3, :, cols[j]] = pair_sum(3, j).astype(BF16)
        x_copy(3, j).start()

    def stage_pass(j):
        c = cols[j]
        x_copy(0, j).wait_recv()
        own[1, top, c] = (own[1, top, c].astype(F32) + opp_top[:, c].astype(F32)).astype(BF16)
        x_copy(4, j).start()
        x_copy(1, j).wait_recv()
        own[3, bot, c] = (own[3, bot, c].astype(F32) + opp_bot[:, c].astype(F32)).astype(BF16)
        x_copy(5, j).start()

    def stage_low(j):
        c = cols[j]
        total = pair_sum(0, j)
        for k in (2, 3, 4, 5):
            x_copy(k, j).wait_recv()
        total = (total + from_m[:, c].astype(F32) + from_p[:, c].astype(F32)).astype(BF16)
        own[0, :, c] = total
        low_part[:, :, c] = dot(p_t[...], total).astype(BF16).reshape(N_FSDP, -1, WIDTHS[j])
        to_fsdp(lambda to: low_part.at[to, :, c], low_in.at[f, :, c], low_ssem.at[j], low_rsem.at[j], j == steps - 1)

    def stage_adam(j):
        c = cols[j]
        low_in[f, :, c] = low_part[f, :, c]
        wait_bytes(low_in.at[pl.ds(0, N_FSDP - 1), :, c], low_rsem.at[j])
        low = jnp.sum(low_in[:, :, c].astype(F32), axis=0)
        low_all[f, :, c] = low.astype(BF16)
        to_fsdp(lambda to: low_all.at[f, :, c], low_all.at[f, :, c], all_ssem.at[j], all_rsem.at[j], j == steps - 1)
        one = 0.9 * m_buf[:, c] + 0.1 * low
        two = 0.999 * v_buf[:, c] + 0.001 * low * low
        m_buf[:, c] = one
        v_buf[:, c] = two
        norm_all[f, :, c] = (one / (jnp.sqrt(two) + 1e-08)).astype(BF16)

    def stage_norm(j):
        c = cols[j]
        to_fsdp(lambda to: norm_all.at[f, :, c], norm_all.at[f, :, c], norm_ssem.at[j], norm_rsem.at[j])

    def stage_tangent(j):
        c = cols[j]
        wait_bytes(low_all.at[pl.ds(0, N_FSDP - 1), :, c], all_rsem.at[j])
        low = low_all[:, :, c].reshape(rank, WIDTHS[j])
        resid = (own[0, :, c].astype(F32) - dot(p_bf[...], low)).astype(BF16)
        if j == 0:
            tan_acc[...] = dot_nt(resid, low)
        else:
            tan_acc[...] += dot_nt(resid, low)

    def weight_copy(j):
        return pltpu.make_async_copy(w_buf.at[:, cols[j]], new_weight.at[:, cols[j]], out_sem.at[j])

    def stage_weight(j):
        c = cols[j]
        wait_bytes(norm_all.at[pl.ds(0, N_FSDP - 1), :, c], norm_rsem.at[j])
        update = dot(p_bf[...], norm_all[:, :, c].reshape(rank, WIDTHS[j]))
        w_buf[:, c] = (w_buf[:, c].astype(F32) - 2.0 * update).astype(BF16)
        weight_copy(j).start()

    start_sib(0)
    for j in range(1, AHEAD):
        start_loads(j)
        start_sib(j)
    for copy in loads[1:]:
        copy.start()
    loads[0].wait()
    p_bf[...] = p_buf[...].astype(BF16)
    p_t[...] = dot_nt(diagonal((rank, rank), 0, 0).astype(BF16), p_bf[...]).astype(BF16)

    stage_opposite(0)
    for t in range(steps + 3):
        if t + AHEAD < steps:
            start_loads(t + AHEAD)
            start_sib(t + AHEAD)
        if t + 1 < steps:
            stage_opposite(t + 1)
        if t < steps:
            stage_pair(t)
        if t < steps:
            stage_pass(t)
        if t == 1:
            for copy in loads[1:]:
                copy.wait()
        if 1 <= t < steps + 1:
            stage_low(t - 1)
        if 2 <= t < steps + 2:
            stage_adam(t - 2)
        if 3 <= t:
            stage_tangent(t - 3)
            if t - 3 < NORM_EARLY:
                stage_norm(t - 3)
        if 5 <= t < NORM_EARLY + 5:
            stage_weight(t - 5)

    tan_send[...] = tan_acc[...].astype(BF16).reshape(N_X, 2, tan_rows, rank)
    pair_copy = remote(tan_send.at[:, 1 - core], tan_sib, tail_ssem.at[0], tail_rsem.at[0], sib)
    pair_copy.start()
    pair_copy.wait_recv()
    tan_x[...] = (tan_send[:, core].astype(F32) + tan_sib[...].astype(F32)).astype(BF16)
    to_x(lambda to: tan_x.at[to], tan_in.at[x], tail_ssem.at[1], tail_rsem.at[1])
    tan_in[x] = tan_x[x]
    for j in range(NORM_EARLY, steps):
        stage_norm(j)
    outs = [
        pltpu.make_async_copy(m_buf, moment_one, out_sem.at[steps]),
        pltpu.make_async_copy(v_buf, moment_two, out_sem.at[steps + 1]),
    ]
    for copy in outs:
        copy.start()
    wait_bytes(tan_in.at[pl.ds(0, N_X - 1)], tail_rsem.at[1])
    tan_all[x, core] = jnp.sum(tan_in[...].astype(F32), axis=0).astype(BF16)
    to_x(lambda to: tan_all.at[x, core], tan_all.at[x, core], tail_ssem.at[2], tail_rsem.at[2])

    for j in range(NORM_EARLY, NORM_EARLY + 2):
        stage_weight(j)
    proj_sq = fold_rows(p_buf[...] * p_buf[...])
    pick = diagonal((tan_rows, rank), d * tan_rows, 0).astype(BF16)
    proj_pick = dot_nt(pick, p_bf[...]).astype(BF16)

    wait_bytes(tan_all.at[pl.ds(0, N_X - 1), 0], tail_rsem.at[2])
    pair_all = remote(tan_all.at[:, core], tan_all.at[:, core], tail_ssem.at[3], tail_rsem.at[3], sib)
    pair_all.start()
    pair_all.wait_recv()

    tan = tan_all[...].reshape(rank, rank)
    tan_copy = pltpu.make_async_copy(tan_all, tan_out, out_sem.at[steps + 2])
    tan_copy.start()
    tan_pick = dot_nt(pick, tan).astype(BF16)
    picks = jnp.concatenate([proj_pick, tan_pick], axis=0)
    with_proj = dot(picks, p_bf[...])
    with_tan = dot(picks, tan)
    gram_pp = with_proj[:tan_rows]
    gram_pt = with_proj[tan_rows:] + with_tan[:tan_rows]
    gram_tt = with_tan[tan_rows:]
    tan_f = tan.astype(F32)
    stats = jnp.concatenate([fold_rows(tan_f * tan_f), proj_sq], axis=0).astype(BF16)
    for to_y in range(4):
        for to_z in range(4):
            block = (slice(16 * to_y, 16 * to_y + 16), slice(128 * to_z, 128 * to_z + 128))
            at = 4 * to_y + to_z
            gram_send[at, 0:16] = gram_pp[block].astype(BF16)
            gram_send[at, 16:32] = gram_pt[block].astype(BF16)
            gram_send[at, 32:48] = gram_tt[block].astype(BF16)
            gram_send[at, 48:64] = stats
    to_fsdp(lambda to: gram_send.at[to], gram_in.at[f], tail_ssem.at[4], tail_rsem.at[4], True)
    gram_in[f] = gram_send[f]
    for j in range(NORM_EARLY + 2, steps):
        stage_weight(j)
    for j in range(steps):
        c = cols[j]
        for q in range(N_X):
            sib_copy(q, j).wait_send()
        for k in range(6):
            x_copy(k, j).wait_send()
        wait_bytes(low_in.at[pl.ds(0, N_FSDP - 1), :, c], low_ssem.at[j])
        wait_bytes(low_all.at[pl.ds(0, N_FSDP - 1), :, c], all_ssem.at[j])
        wait_bytes(norm_all.at[pl.ds(0, N_FSDP - 1), :, c], norm_ssem.at[j])
    wait_bytes(gram_in.at[pl.ds(0, N_FSDP - 1)], tail_rsem.at[4])
    sums = jnp.sum(gram_in[...].astype(F32), axis=0)
    tan_total = jnp.sum(sums[48:56])
    proj_total = jnp.sum(sums[56:64])
    tan_scale = 0.5 * jnp.sqrt(F32(rank)) / jnp.sqrt(jnp.full((1, 1), tan_total, F32) + 1e-06)
    middle = (proj_total + tan_scale * tan_scale * tan_total) / rank
    block = sums[0:16] + tan_scale * sums[16:32] + tan_scale * tan_scale * sums[32:48]
    on_diagonal = diagonal((16, 128), d * tan_rows + y * 16, z * 128)
    gram_all[x, core, f] = (block - jnp.where(on_diagonal, middle, 0.0)).astype(BF16)
    mine = gram_all.at[x, core, f]

    for at in chips:
        remote(mine, mine, tail_ssem.at[5], tail_rsem.at[5], chip_at(at)).start()

    scale_buf[0:8] = jnp.broadcast_to(tan_scale, (8, 128))
    scale_buf[8:16] = jnp.broadcast_to(middle, (8, 128))
    scale_copy = pltpu.make_async_copy(scale_buf, scale_out, out_sem.at[steps + 3])
    scale_copy.start()
    pair_copy.wait_send()
    wait_bytes(tan_in.at[pl.ds(0, N_X - 1)], tail_ssem.at[1])
    wait_bytes(tan_all.at[pl.ds(0, N_X - 1), 0], tail_ssem.at[2])
    pair_all.wait_send()
    wait_bytes(gram_in.at[pl.ds(0, N_FSDP - 1)], tail_ssem.at[4])
    for copy in outs:
        copy.wait()
    for j in range(steps):
        weight_copy(j).wait()
    tan_copy.wait()
    blocks = own.at[0, pl.ds(0, 144), pl.ds(0, 896)]
    wait_bytes(blocks, tail_rsem.at[5])
    pair_gram = remote(gram_all.at[:, core], gram_all.at[:, core], tail_ssem.at[7], tail_rsem.at[7], sib)
    pair_gram.start()
    pair_gram.wait_recv()
    gram_copy = pltpu.make_async_copy(gram_all, gram_out, out_sem.at[steps + 4])
    gram_copy.start()

    wait_bytes(blocks, tail_ssem.at[5])
    pair_gram.wait_send()
    scale_copy.wait()
    gram_copy.wait()


def finish_kernel(
    weight_in, one_in, two_in, tan, gram, scale, proj,
    new_weight, new_proj, moment_one, moment_two,
    tan_buf, gram_buf, scale_buf, proj_buf, w_state, q_state, out_buf, weight_buf, one_buf, two_buf, sems,
):
    rank = proj.shape[1]
    copies = [
        pltpu.make_async_copy(gram, gram_buf, sems.at[0]),
        pltpu.make_async_copy(scale, scale_buf, sems.at[1]),
        pltpu.make_async_copy(tan, tan_buf, sems.at[2]),
        pltpu.make_async_copy(proj, proj_buf, sems.at[3]),
        pltpu.make_async_copy(weight_in, weight_buf, sems.at[4]),
        pltpu.make_async_copy(one_in, one_buf, sems.at[5]),
        pltpu.make_async_copy(two_in, two_buf, sems.at[6]),
    ]
    passed = [
        pltpu.make_async_copy(weight_buf, new_weight, sems.at[4]),
        pltpu.make_async_copy(one_buf, moment_one, sems.at[5]),
        pltpu.make_async_copy(two_buf, moment_two, sems.at[6]),
    ]
    for copy in copies:
        copy.start()
    copies[0].wait()
    copies[1].wait()
    tan_scale = scale_buf[0:1, 0:1]
    middle = scale_buf[8:9, 0:1]
    eye = diagonal((rank, rank), 0, 0)
    whole = gram_buf[...].astype(F32).reshape(N_DP, 4, 4, 16, 128)
    gram_dev = jnp.concatenate([whole[:, :, at].reshape(rank, 128) for at in range(4)], axis=1)
    trace_dev = jnp.sum(jnp.sum(jnp.where(eye, gram_dev, 0.0), axis=0, keepdims=True), axis=1, keepdims=True)
    frame_sq = trace_dev + rank * middle + 1e-06
    inverse = 1.0 / frame_sq
    shift = trace_dev / rank
    center = (middle + shift) * inverse
    state = (gram_dev - jnp.where(eye, shift, 0.0)) * inverse
    w_state[...] = state
    q_center = None
    for sweep in range(NS_ITERS):
        state = w_state[...]
        state_b = state.astype(BF16)
        poly = (COEF_B + 2.0 * COEF_C * center) * state + COEF_C * dot(state_b, state_b)
        poly_center = COEF_A + COEF_B * center + COEF_C * center * center
        poly_b = poly.astype(BF16)
        if sweep == 0:
            q_state[...] = poly
            q_center = poly_center
        else:
            q_now = q_state[...]
            q_state[...] = q_center * poly + poly_center * q_now + dot(q_now.astype(BF16), poly_b)
            q_center = q_center * poly_center
        if sweep == 0:
            for copy, on in zip(copies[4:], passed):
                copy.wait()
                on.start()
        if sweep < NS_ITERS - 1:
            once = center * poly + poly_center * state + dot(state_b, poly_b)
            once_center = center * poly_center
            w_state[...] = once_center * poly + poly_center * once + dot(once.astype(BF16), poly_b)
            center = once_center * poly_center
    q_now = q_state[...]
    q_shift = jnp.sum(jnp.sum(jnp.where(eye, q_now, 0.0), axis=0, keepdims=True), axis=1, keepdims=True) / rank
    q_b = (q_now - jnp.where(eye, q_shift, 0.0)).astype(BF16)
    copies[2].wait()
    copies[3].wait()
    scale_down = 1.0 / jnp.sqrt(frame_sq)
    frame = (proj_buf[...] + tan_scale * tan_buf[...].reshape(rank, rank).astype(F32)) * scale_down
    out_buf[...] = (q_center + q_shift) * frame + dot(frame.astype(BF16), q_b)
    last = pltpu.make_async_copy(out_buf, new_proj, sems.at[7])
    last.start()
    for copy in passed:
        copy.wait()
    last.wait()


def on_device(grad_parts, weight, projector, exp_avg, exp_avg_sq):
    grad = grad_parts.reshape(grad_parts.shape[1:])
    rows = grad.shape[0]
    rank = projector.shape[1]
    share, owned = exp_avg.shape
    steps = len(WIDTHS)
    tan_rows = rank // N_DP
    vmem = pltpu.VMEM
    dma = pltpu.SemaphoreType.DMA
    hbm = pl.BlockSpec(memory_space=pl.ANY)
    shape = jax.ShapeDtypeStruct
    tan_shape = (N_X, 2, tan_rows, rank)
    gram_shape = (N_X, 2, N_FSDP, 16, 128)
    mid = pl.pallas_call(
        kernel,
        out_shape=(
            shape(weight.shape, weight.dtype),
            shape(exp_avg.shape, F32),
            shape(exp_avg_sq.shape, F32),
            shape(tan_shape, BF16),
            shape(gram_shape, BF16),
            shape((16, 128), F32),
        ),
        in_specs=[hbm] * 5,
        out_specs=(hbm,) * 6,
        scratch_shapes=[
            vmem((N_X, rows, owned), BF16),
            vmem((N_X, rows, owned), BF16),
            vmem((rows // 2, owned), BF16),
            vmem((rows // 2, owned), BF16),
            vmem((rows, owned), BF16),
            vmem((rows, owned), BF16),
            vmem((N_FSDP, share, owned), BF16),
            vmem((N_FSDP, share, owned), BF16),
            vmem((N_FSDP, share, owned), BF16),
            vmem((N_FSDP, share, owned), BF16),
            vmem(weight.shape, BF16),
            vmem(projector.shape, F32),
            vmem(exp_avg.shape, F32),
            vmem(exp_avg_sq.shape, F32),
            vmem(projector.shape, BF16),
            vmem((rank, rows), BF16),
            vmem((rows, rank), F32),
            vmem(tan_shape, BF16),
            vmem((N_X, tan_rows, rank), BF16),
            vmem((N_X, tan_rows, rank), BF16),
            vmem((N_X, tan_rows, rank), BF16),
            vmem(tan_shape, BF16),
            vmem((N_FSDP, 64, 128), BF16),
            vmem((N_FSDP, 64, 128), BF16),
            vmem(gram_shape, BF16),
            vmem((16, 128), F32),
            dma((4,)),
            dma((steps, N_X)),
            dma((steps, N_X)),
            dma((steps, N_X)),
            dma((steps, 6)),
            dma((steps, 6)),
            dma((steps,)),
            dma((steps,)),
            dma((steps,)),
            dma((steps,)),
            dma((steps,)),
            dma((steps,)),
            dma((8,)),
            dma((8,)),
            dma((steps + 5,)),
        ],
        compiler_params=pltpu.CompilerParams(
            collective_id=0, has_side_effects=True, vmem_limit_bytes=60 * 1024 * 1024
        ),
    )(grad, weight, projector, exp_avg, exp_avg_sq)
    return pl.pallas_call(
        finish_kernel,
        out_shape=(
            shape(weight.shape, weight.dtype),
            shape(projector.shape, F32),
            shape(exp_avg.shape, F32),
            shape(exp_avg_sq.shape, F32),
        ),
        in_specs=[hbm] * 7,
        out_specs=(hbm,) * 4,
        scratch_shapes=[
            vmem(tan_shape, BF16),
            vmem(gram_shape, BF16),
            vmem((16, 128), F32),
            vmem(projector.shape, F32),
            vmem((rank, rank), F32),
            vmem((rank, rank), F32),
            vmem(projector.shape, F32),
            vmem(weight.shape, BF16),
            vmem(exp_avg.shape, F32),
            vmem(exp_avg_sq.shape, F32),
            dma((8,)),
        ],
        compiler_params=pltpu.CompilerParams(vmem_limit_bytes=60 * 1024 * 1024),
    )(*mid, projector)


def solution(mesh):
    return jax.shard_map(
        on_device,
        mesh=mesh,
        in_specs=(
            P("dp", "fsdp", None),
            P("fsdp", "dp"),
            P("fsdp", None),
            P("fsdp", "dp"),
            P("fsdp", "dp"),
        ),
        out_specs=(P("fsdp", "dp"), P("fsdp", None), P("fsdp", "dp"), P("fsdp", "dp")),
        check_vma=False,
    )
```

```python
import jax
import jax.numpy as jnp
from jax import lax
from jax.experimental import pallas as pl
from jax.experimental.pallas import tpu as pltpu
from jax.sharding import PartitionSpec as P

NS_ITERS = 5

COEF_A = 3.4445
COEF_B = -4.775
COEF_C = 2.0315

MESH = pl.DeviceIdType.MESH
BF16 = jnp.bfloat16
F32 = jnp.float32

N_X = 4
N_DP = 8
N_FSDP = 16
N_CHIPS = N_X * N_FSDP
WIDTHS = (256,) * 7
AHEAD = 2
NORM_EARLY = 3
TAN_PARTS = 2


def dot(left, right):
    return jnp.dot(left, right, preferred_element_type=F32)


def dot_nt(left, right):
    return lax.dot_general(left, right, (((1,), (1,)), ((), ())), preferred_element_type=F32)


def diagonal(shape, row_at, col_at):
    rows = lax.broadcasted_iota(jnp.int32, shape, 0) + row_at
    cols = lax.broadcasted_iota(jnp.int32, shape, 1) + col_at
    return rows == cols


def fold_rows(value):
    rows, cols = value.shape
    part = jnp.sum(value.reshape(rows // 8, 8, cols), axis=0)
    total = part[:, 0:128]
    for at in range(128, cols, 128):
        total = total + part[:, at : at + 128]
    return total


def kernel(
    grad, weight, proj, avg, avg_sq,
    new_weight, moment_one, moment_two, tan_out, gram_out, scale_out,
    own, sib_in, opp_top, opp_bot, from_m, from_p,
    low_part, low_in, low_all, norm_all,
    w_buf, p_buf, m_buf, v_buf, p_bf, p_t, tan_acc,
    tan_send, tan_sib, tan_x, tan_in, tan_all, base_send, base_in, proj_pick, gram_send, gram_in, gram_all, scale_buf,
    load_sem, own_sem, sib_ssem, sib_rsem, x_ssem, x_rsem,
    low_ssem, low_rsem, all_ssem, all_rsem, norm_ssem, norm_rsem, tan_ssem, tan_rsem, tail_ssem, tail_rsem, out_sem,
):
    rows = grad.shape[0]
    rank = proj.shape[1]
    owned = avg.shape[1]
    steps = len(WIDTHS)
    half = rows // 2
    tan_rows = rank // N_DP

    d = lax.axis_index("dp")
    f = lax.axis_index("fsdp")
    x, core = lax.div(d, 2), lax.rem(d, 2)
    y, z = lax.div(f, 4), lax.rem(f, 4)
    xs = [lax.rem(x + i, N_X) for i in range(N_X)]
    ys = [lax.rem(y + i, 4) for i in range(4)]
    zs = [lax.rem(z + i, 4) for i in range(4)]
    far = (2, 1, 3, 0)
    hops = (0, 1, 2, 1)
    sib = {"dp": 2 * x + (1 - core)}
    right = {"dp": 2 * xs[1] + core}
    left = {"dp": 2 * xs[3] + core}

    def remote(src, dst, ssem, rsem, device):
        return pltpu.make_async_remote_copy(
            src_ref=src, dst_ref=dst, send_sem=ssem, recv_sem=rsem, device_id=device, device_id_type=MESH
        )

    def wait_bytes(ref, sem):
        pltpu.make_async_copy(ref, ref, sem).wait()

    planes = sorted(((i, j) for i in range(4) for j in range(4)), key=lambda at: -hops[at[0]] - hops[at[1]])[:-1]
    chips = sorted(
        ((k, i, j) for k in range(4) for i in range(4) for j in range(4)),
        key=lambda at: -hops[at[0]] - hops[at[1]] - hops[at[2]],
    )[:-1]

    def to_fsdp(src_of, dst, ssem, rsem, ordered=False):
        if ordered:
            for i, j in planes:
                to = 4 * ys[i] + zs[j]
                remote(src_of(to), dst, ssem, rsem, {"fsdp": to}).start()
            return

        @pl.loop(1, N_FSDP)
        def _(i):
            to = lax.rem(f + i, N_FSDP)
            remote(src_of(to), dst, ssem, rsem, {"fsdp": to}).start()

    def to_x(src_of, dst, ssem, rsem):
        for i in far[:3]:
            to = xs[i]
            remote(src_of(to), dst, ssem, rsem, {"dp": 2 * to + core}).start()

    def chip_at(at):
        return {"dp": 2 * xs[at[0]] + core, "fsdp": 4 * ys[at[1]] + zs[at[2]]}

    starts = [sum(WIDTHS[:j]) for j in range(steps)]
    cols = [pl.ds(starts[j], WIDTHS[j]) for j in range(steps)]

    def columns(owner, j):
        return pl.ds(pl.multiple_of(owner * owned + starts[j], 128), WIDTHS[j])

    def own_copy(q, j):
        return pltpu.make_async_copy(
            grad.at[:, columns(2 * xs[q] + core, j)], own.at[q, :, cols[j]], own_sem.at[j, q]
        )

    def sib_copy(q, j):
        return remote(
            grad.at[:, columns(2 * xs[q] + (1 - core), j)],
            sib_in.at[q, :, cols[j]], sib_ssem.at[j, q], sib_rsem.at[j, q], sib,
        )

    top, bot = pl.ds(0, half), pl.ds(half, half)

    def x_copy(k, j):
        c = cols[j]
        src, dst, device = (
            (own.at[2, top, c], opp_top.at[:, c], right),
            (own.at[2, bot, c], opp_bot.at[:, c], left),
            (own.at[1, bot, c], from_m.at[bot, c], right),
            (own.at[3, top, c], from_p.at[top, c], left),
            (own.at[1, top, c], from_m.at[top, c], right),
            (own.at[3, bot, c], from_p.at[bot, c], left),
        )[k]
        return remote(src, dst, x_ssem.at[j, k], x_rsem.at[j, k], device)

    loads = [
        pltpu.make_async_copy(proj, p_buf, load_sem.at[0]),
        pltpu.make_async_copy(avg, m_buf, load_sem.at[1]),
        pltpu.make_async_copy(avg_sq, v_buf, load_sem.at[2]),
        pltpu.make_async_copy(weight, w_buf, load_sem.at[3]),
    ]

    def start_loads(j):
        for q in (2, 1, 3, 0):
            own_copy(q, j).start()

    def start_sib(j):
        for q in (2, 1, 3, 0):
            sib_copy(q, j).start()

    loads[0].start()
    start_loads(0)
    barrier = pltpu.get_barrier_semaphore()
    pl.semaphore_signal(barrier, inc=1, device_id=sib, device_id_type=MESH)
    for i in range(1, N_CHIPS):
        to = lax.rem(x * N_FSDP + f + i, N_CHIPS)
        device = {"dp": 2 * lax.div(to, N_FSDP) + core, "fsdp": lax.rem(to, N_FSDP)}
        pl.semaphore_signal(barrier, inc=1, device_id=device, device_id_type=MESH)
    pl.semaphore_wait(barrier, N_CHIPS)

    def pair_sum(q, j):
        own_copy(q, j).wait()
        sib_copy(q, j).wait_recv()
        return own[q, :, cols[j]].astype(F32) + sib_in[q, :, cols[j]].astype(F32)

    def stage_opposite(j):
        own[2, :, cols[j]] = pair_sum(2, j).astype(BF16)
        x_copy(0, j).start()
        x_copy(1, j).start()

    def stage_pair(j):
        own[1, :, cols[j]] = pair_sum(1, j).astype(BF16)
        x_copy(2, j).start()
        own[3, :, cols[j]] = pair_sum(3, j).astype(BF16)
        x_copy(3, j).start()

    def stage_pass(j):
        c = cols[j]
        x_copy(0, j).wait_recv()
        own[1, top, c] = (own[1, top, c].astype(F32) + opp_top[:, c].astype(F32)).astype(BF16)
        x_copy(4, j).start()
        x_copy(1, j).wait_recv()
        own[3, bot, c] = (own[3, bot, c].astype(F32) + opp_bot[:, c].astype(F32)).astype(BF16)
        x_copy(5, j).start()

    def stage_low(j):
        c = cols[j]
        total = pair_sum(0, j)
        for k in (2, 3, 4, 5):
            x_copy(k, j).wait_recv()
        total = (total + from_m[:, c].astype(F32) + from_p[:, c].astype(F32)).astype(BF16)
        own[0, :, c] = total
        low_part[:, :, c] = dot(p_t[...], total).astype(BF16).reshape(N_FSDP, -1, WIDTHS[j])
        to_fsdp(lambda to: low_part.at[to, :, c], low_in.at[f, :, c], low_ssem.at[j], low_rsem.at[j], j == steps - 1)

    def stage_adam(j):
        c = cols[j]
        low_in[f, :, c] = low_part[f, :, c]
        wait_bytes(low_in.at[pl.ds(0, N_FSDP - 1), :, c], low_rsem.at[j])
        low = jnp.sum(low_in[:, :, c].astype(F32), axis=0)
        low_all[f, :, c] = low.astype(BF16)
        to_fsdp(lambda to: low_all.at[f, :, c], low_all.at[f, :, c], all_ssem.at[j], all_rsem.at[j], j == steps - 1)
        one = 0.9 * m_buf[:, c] + 0.1 * low
        two = 0.999 * v_buf[:, c] + 0.001 * low * low
        m_buf[:, c] = one
        v_buf[:, c] = two
        norm_all[f, :, c] = (one / (jnp.sqrt(two) + 1e-08)).astype(BF16)

    def stage_norm(j):
        c = cols[j]
        to_fsdp(lambda to: norm_all.at[f, :, c], norm_all.at[f, :, c], norm_ssem.at[j], norm_rsem.at[j])

    def stage_tangent(j):
        c = cols[j]
        wait_bytes(low_all.at[pl.ds(0, N_FSDP - 1), :, c], all_rsem.at[j])
        low = low_all[:, :, c].reshape(rank, WIDTHS[j])
        resid = (own[0, :, c].astype(F32) - dot(p_bf[...], low)).astype(BF16)
        if j == 0:
            tan_acc[...] = dot_nt(resid, low)
        else:
            tan_acc[...] += dot_nt(resid, low)

    def weight_copy(j):
        return pltpu.make_async_copy(w_buf.at[:, cols[j]], new_weight.at[:, cols[j]], out_sem.at[j])

    def stage_weight(j):
        c = cols[j]
        wait_bytes(norm_all.at[pl.ds(0, N_FSDP - 1), :, c], norm_rsem.at[j])
        update = dot(p_bf[...], norm_all[:, :, c].reshape(rank, WIDTHS[j]))
        w_buf[:, c] = (w_buf[:, c].astype(F32) - 2.0 * update).astype(BF16)
        weight_copy(j).start()

    pick = diagonal((tan_rows, rank), d * tan_rows, 0).astype(BF16)

    def send_proj_gram():
        proj_pick[...] = dot_nt(pick, p_bf[...]).astype(BF16)
        gram_pp = dot(proj_pick[...], p_bf[...])
        proj_sq = fold_rows(p_buf[...] * p_buf[...])
        proj_sq = jnp.concatenate([proj_sq, jnp.zeros_like(proj_sq)], axis=0).astype(BF16)
        for to_y in range(4):
            for to_z in range(4):
                block = gram_pp[16 * to_y : 16 * to_y + 16, 128 * to_z : 128 * to_z + 128]
                base_send[4 * to_y + to_z, 0:16] = block.astype(BF16)
                base_send[4 * to_y + to_z, 16:32] = proj_sq
        to_fsdp(lambda to: base_send.at[to], base_in.at[f], tail_ssem.at[6], tail_rsem.at[6])
        base_in[f] = base_send[f]

    start_sib(0)
    stage_opposite(0)
    for j in range(1, AHEAD):
        start_loads(j)
        start_sib(j)
    stage_pair(0)
    for copy in loads[1:]:
        copy.start()
    loads[0].wait()
    p_bf[...] = p_buf[...].astype(BF16)
    p_t[...] = dot_nt(diagonal((rank, rank), 0, 0).astype(BF16), p_bf[...]).astype(BF16)

    for t in range(steps + 3):
        if t + AHEAD < steps:
            start_loads(t + AHEAD)
            start_sib(t + AHEAD)
        if t + 1 < steps:
            stage_opposite(t + 1)
        if 0 < t < steps:
            stage_pair(t)
        if t < steps:
            stage_pass(t)
        if t == 1:
            for copy in loads[1:]:
                copy.wait()
            send_proj_gram()
        if 1 <= t < steps + 1:
            stage_low(t - 1)
        if 2 <= t < steps + 2:
            stage_adam(t - 2)
        if 3 <= t:
            stage_tangent(t - 3)
            if t - 3 < NORM_EARLY:
                stage_norm(t - 3)
        if 5 <= t < NORM_EARLY + 5:
            stage_weight(t - 5)

    tan_send[...] = tan_acc[...].astype(BF16).reshape(N_X, 2, tan_rows, rank)
    pair_copy = remote(tan_send.at[:, 1 - core], tan_sib, tail_ssem.at[0], tail_rsem.at[0], sib)
    pair_copy.start()
    stage_norm(NORM_EARLY)
    pair_copy.wait_recv()
    parts = [pl.ds(k * (rank // TAN_PARTS), rank // TAN_PARTS) for k in range(TAN_PARTS)]
    for k, c in enumerate(parts):
        tan_x[:, :, c] = (tan_send[:, core, :, c].astype(F32) + tan_sib[:, :, c].astype(F32)).astype(BF16)
        to_x(lambda to: tan_x.at[to, :, c], tan_in.at[x, :, c], tan_ssem.at[0, k], tan_rsem.at[0, k])
        tan_in[x, :, c] = tan_x[x, :, c]
    for j in range(NORM_EARLY + 1, steps - 1):
        stage_norm(j)
    for k, c in enumerate(parts):
        wait_bytes(tan_in.at[pl.ds(0, N_X - 1), :, c], tan_rsem.at[0, k])
        tan_all[x, core, :, c] = jnp.sum(tan_in[:, :, c].astype(F32), axis=0).astype(BF16)
        mine = tan_all.at[x, core, :, c]
        to_x(lambda to: mine, mine, tan_ssem.at[1, k], tan_rsem.at[1, k])
    stage_norm(steps - 1)
    outs = [
        pltpu.make_async_copy(m_buf, moment_one, out_sem.at[steps]),
        pltpu.make_async_copy(v_buf, moment_two, out_sem.at[steps + 1]),
    ]
    for copy in outs:
        copy.start()
    for j in range(NORM_EARLY, NORM_EARLY + 2):
        stage_weight(j)
    pair_all = []
    for k, c in enumerate(parts):
        wait_bytes(tan_all.at[pl.ds(0, N_X - 1), 0, :, c], tan_rsem.at[1, k])
        mine = tan_all.at[:, core, :, c]
        pair_all.append(remote(mine, mine, tan_ssem.at[2, k], tan_rsem.at[2, k], sib))
        pair_all[k].start()
    for copy in pair_all:
        copy.wait_recv()

    tan = tan_all[...].reshape(rank, rank)
    tan_copy = pltpu.make_async_copy(tan_all, tan_out, out_sem.at[steps + 2])
    tan_copy.start()
    tan_pick = dot_nt(pick, tan).astype(BF16)
    with_tan = dot(jnp.concatenate([proj_pick[...], tan_pick], axis=0), tan)
    gram_pt = dot(tan_pick, p_bf[...]) + with_tan[:tan_rows]
    gram_tt = with_tan[tan_rows:]
    tan_f = tan.astype(F32)
    tan_sq = fold_rows(tan_f * tan_f)
    stats = jnp.concatenate([tan_sq, jnp.zeros_like(tan_sq)], axis=0).astype(BF16)
    for to_y in range(4):
        for to_z in range(4):
            block = (slice(16 * to_y, 16 * to_y + 16), slice(128 * to_z, 128 * to_z + 128))
            at = 4 * to_y + to_z
            gram_send[at, 0:16] = gram_pt[block].astype(BF16)
            gram_send[at, 16:32] = gram_tt[block].astype(BF16)
            gram_send[at, 32:48] = stats
    to_fsdp(lambda to: gram_send.at[to], gram_in.at[f], tail_ssem.at[4], tail_rsem.at[4], True)
    gram_in[f] = gram_send[f]
    for j in range(NORM_EARLY + 2, steps):
        stage_weight(j)
    for j in range(steps):
        c = cols[j]
        for q in range(N_X):
            sib_copy(q, j).wait_send()
        for k in range(6):
            x_copy(k, j).wait_send()
        wait_bytes(low_in.at[pl.ds(0, N_FSDP - 1), :, c], low_ssem.at[j])
        wait_bytes(low_all.at[pl.ds(0, N_FSDP - 1), :, c], all_ssem.at[j])
        wait_bytes(norm_all.at[pl.ds(0, N_FSDP - 1), :, c], norm_ssem.at[j])
    wait_bytes(base_in.at[pl.ds(0, N_FSDP - 1)], tail_rsem.at[6])
    base = jnp.sum(base_in[...].astype(F32), axis=0)
    proj_total = jnp.sum(base[16:32])
    wait_bytes(gram_in.at[pl.ds(0, N_FSDP - 1)], tail_rsem.at[4])
    sums = jnp.sum(gram_in[...].astype(F32), axis=0)
    tan_total = jnp.sum(sums[32:40])
    tan_scale = 0.5 * jnp.sqrt(F32(rank)) / jnp.sqrt(jnp.full((1, 1), tan_total, F32) + 1e-06)
    middle = (proj_total + tan_scale * tan_scale * tan_total) / rank
    block = base[0:16] + tan_scale * sums[0:16] + tan_scale * tan_scale * sums[16:32]
    on_diagonal = diagonal((16, 128), d * tan_rows + y * 16, z * 128)
    gram_all[x, core, f] = (block - jnp.where(on_diagonal, middle, 0.0)).astype(BF16)
    mine = gram_all.at[x, core, f]

    for at in chips:
        remote(mine, mine, tail_ssem.at[5], tail_rsem.at[5], chip_at(at)).start()

    scale_buf[0:8] = jnp.broadcast_to(tan_scale, (8, 128))
    scale_buf[8:16] = jnp.broadcast_to(middle, (8, 128))
    scale_copy = pltpu.make_async_copy(scale_buf, scale_out, out_sem.at[steps + 3])
    scale_copy.start()
    wait_bytes(base_in.at[pl.ds(0, N_FSDP - 1)], tail_ssem.at[6])
    pair_copy.wait_send()
    for k, c in enumerate(parts):
        wait_bytes(tan_in.at[pl.ds(0, N_X - 1), :, c], tan_ssem.at[0, k])
        wait_bytes(tan_all.at[pl.ds(0, N_X - 1), 0, :, c], tan_ssem.at[1, k])
        pair_all[k].wait_send()
    wait_bytes(gram_in.at[pl.ds(0, N_FSDP - 1)], tail_ssem.at[4])
    for copy in outs:
        copy.wait()
    for j in range(steps):
        weight_copy(j).wait()
    tan_copy.wait()
    blocks = own.at[0, pl.ds(0, 144), pl.ds(0, 896)]
    wait_bytes(blocks, tail_rsem.at[5])
    pair_gram = remote(gram_all.at[:, core], gram_all.at[:, core], tail_ssem.at[7], tail_rsem.at[7], sib)
    pair_gram.start()
    pair_gram.wait_recv()
    gram_copy = pltpu.make_async_copy(gram_all, gram_out, out_sem.at[steps + 4])
    gram_copy.start()

    wait_bytes(blocks, tail_ssem.at[5])
    pair_gram.wait_send()
    scale_copy.wait()
    gram_copy.wait()


def finish_kernel(
    weight_in, one_in, two_in, tan, gram, scale, proj,
    new_weight, new_proj, moment_one, moment_two,
    tan_buf, gram_buf, scale_buf, proj_buf, w_state, q_state, out_buf, weight_buf, one_buf, two_buf, sems,
):
    rank = proj.shape[1]
    copies = [
        pltpu.make_async_copy(gram, gram_buf, sems.at[0]),
        pltpu.make_async_copy(scale, scale_buf, sems.at[1]),
        pltpu.make_async_copy(tan, tan_buf, sems.at[2]),
        pltpu.make_async_copy(proj, proj_buf, sems.at[3]),
        pltpu.make_async_copy(weight_in, weight_buf, sems.at[4]),
        pltpu.make_async_copy(one_in, one_buf, sems.at[5]),
        pltpu.make_async_copy(two_in, two_buf, sems.at[6]),
    ]
    passed = [
        pltpu.make_async_copy(weight_buf, new_weight, sems.at[4]),
        pltpu.make_async_copy(one_buf, moment_one, sems.at[5]),
        pltpu.make_async_copy(two_buf, moment_two, sems.at[6]),
    ]
    for copy in copies:
        copy.start()
    copies[0].wait()
    copies[1].wait()
    tan_scale = scale_buf[0:1, 0:1]
    middle = scale_buf[8:9, 0:1]
    eye = diagonal((rank, rank), 0, 0)
    whole = gram_buf[...].astype(F32).reshape(N_DP, 4, 4, 16, 128)
    gram_dev = jnp.concatenate([whole[:, :, at].reshape(rank, 128) for at in range(4)], axis=1)
    trace_dev = jnp.sum(jnp.sum(jnp.where(eye, gram_dev, 0.0), axis=0, keepdims=True), axis=1, keepdims=True)
    frame_sq = trace_dev + rank * middle + 1e-06
    inverse = 1.0 / frame_sq
    shift = trace_dev / rank
    center = (middle + shift) * inverse
    state = (gram_dev - jnp.where(eye, shift, 0.0)) * inverse
    w_state[...] = state
    q_center = None
    for sweep in range(NS_ITERS):
        state = w_state[...]
        state_b = state.astype(BF16)
        poly = (COEF_B + 2.0 * COEF_C * center) * state + COEF_C * dot(state_b, state_b)
        poly_center = COEF_A + COEF_B * center + COEF_C * center * center
        poly_b = poly.astype(BF16)
        if sweep == 0:
            q_state[...] = poly
            q_center = poly_center
        else:
            q_now = q_state[...]
            q_state[...] = q_center * poly + poly_center * q_now + dot(q_now.astype(BF16), poly_b)
            q_center = q_center * poly_center
        if sweep == 1:
            for copy, on in zip(copies[4:], passed):
                copy.wait()
                on.start()
        if sweep < NS_ITERS - 1:
            once = center * poly + poly_center * state + dot(state_b, poly_b)
            once_center = center * poly_center
            w_state[...] = once_center * poly + poly_center * once + dot(once.astype(BF16), poly_b)
            center = once_center * poly_center
    q_now = q_state[...]
    q_shift = jnp.sum(jnp.sum(jnp.where(eye, q_now, 0.0), axis=0, keepdims=True), axis=1, keepdims=True) / rank
    q_b = (q_now - jnp.where(eye, q_shift, 0.0)).astype(BF16)
    copies[2].wait()
    copies[3].wait()
    scale_down = 1.0 / jnp.sqrt(frame_sq)
    q_all = q_center + q_shift
    last = []
    part = proj_buf.shape[0] // N_X
    for k in range(N_X):
        at = pl.ds(k * part, part)
        frame = (proj_buf[at] + tan_scale * tan_buf[k].reshape(part, rank).astype(F32)) * scale_down
        out_buf[at] = q_all * frame + dot(frame.astype(BF16), q_b)
        last.append(pltpu.make_async_copy(out_buf.at[at], new_proj.at[at], sems.at[7 + k]))
        last[k].start()
    for copy in passed:
        copy.wait()
    for copy in last:
        copy.wait()


def on_device(grad_parts, weight, projector, exp_avg, exp_avg_sq):
    grad = grad_parts.reshape(grad_parts.shape[1:])
    rows = grad.shape[0]
    rank = projector.shape[1]
    share, owned = exp_avg.shape
    steps = len(WIDTHS)
    tan_rows = rank // N_DP
    vmem = pltpu.VMEM
    dma = pltpu.SemaphoreType.DMA
    hbm = pl.BlockSpec(memory_space=pl.ANY)
    shape = jax.ShapeDtypeStruct
    tan_shape = (N_X, 2, tan_rows, rank)
    gram_shape = (N_X, 2, N_FSDP, 16, 128)
    mid = pl.pallas_call(
        kernel,
        out_shape=(
            shape(weight.shape, weight.dtype),
            shape(exp_avg.shape, F32),
            shape(exp_avg_sq.shape, F32),
            shape(tan_shape, BF16),
            shape(gram_shape, BF16),
            shape((16, 128), F32),
        ),
        in_specs=[hbm] * 5,
        out_specs=(hbm,) * 6,
        scratch_shapes=[
            vmem((N_X, rows, owned), BF16),
            vmem((N_X, rows, owned), BF16),
            vmem((rows // 2, owned), BF16),
            vmem((rows // 2, owned), BF16),
            vmem((rows, owned), BF16),
            vmem((rows, owned), BF16),
            vmem((N_FSDP, share, owned), BF16),
            vmem((N_FSDP, share, owned), BF16),
            vmem((N_FSDP, share, owned), BF16),
            vmem((N_FSDP, share, owned), BF16),
            vmem(weight.shape, BF16),
            vmem(projector.shape, F32),
            vmem(exp_avg.shape, F32),
            vmem(exp_avg_sq.shape, F32),
            vmem(projector.shape, BF16),
            vmem((rank, rows), BF16),
            vmem((rows, rank), F32),
            vmem(tan_shape, BF16),
            vmem((N_X, tan_rows, rank), BF16),
            vmem((N_X, tan_rows, rank), BF16),
            vmem((N_X, tan_rows, rank), BF16),
            vmem(tan_shape, BF16),
            vmem((N_FSDP, 32, 128), BF16),
            vmem((N_FSDP, 32, 128), BF16),
            vmem((tan_rows, rank), BF16),
            vmem((N_FSDP, 48, 128), BF16),
            vmem((N_FSDP, 48, 128), BF16),
            vmem(gram_shape, BF16),
            vmem((16, 128), F32),
            dma((4,)),
            dma((steps, N_X)),
            dma((steps, N_X)),
            dma((steps, N_X)),
            dma((steps, 6)),
            dma((steps, 6)),
            dma((steps,)),
            dma((steps,)),
            dma((steps,)),
            dma((steps,)),
            dma((steps,)),
            dma((steps,)),
            dma((3, TAN_PARTS)),
            dma((3, TAN_PARTS)),
            dma((8,)),
            dma((8,)),
            dma((steps + 5,)),
        ],
        compiler_params=pltpu.CompilerParams(
            collective_id=0, has_side_effects=True, vmem_limit_bytes=60 * 1024 * 1024
        ),
    )(grad, weight, projector, exp_avg, exp_avg_sq)
    return pl.pallas_call(
        finish_kernel,
        out_shape=(
            shape(weight.shape, weight.dtype),
            shape(projector.shape, F32),
            shape(exp_avg.shape, F32),
            shape(exp_avg_sq.shape, F32),
        ),
        in_specs=[hbm] * 7,
        out_specs=(hbm,) * 4,
        scratch_shapes=[
            vmem(tan_shape, BF16),
            vmem(gram_shape, BF16),
            vmem((16, 128), F32),
            vmem(projector.shape, F32),
            vmem((rank, rank), F32),
            vmem((rank, rank), F32),
            vmem(projector.shape, F32),
            vmem(weight.shape, BF16),
            vmem(exp_avg.shape, F32),
            vmem(exp_avg_sq.shape, F32),
            dma((11,)),
        ],
        compiler_params=pltpu.CompilerParams(vmem_limit_bytes=60 * 1024 * 1024),
    )(*mid, projector)


def solution(mesh):
    return jax.shard_map(
        on_device,
        mesh=mesh,
        in_specs=(
            P("dp", "fsdp", None),
            P("fsdp", "dp"),
            P("fsdp", None),
            P("fsdp", "dp"),
            P("fsdp", "dp"),
        ),
        out_specs=(P("fsdp", "dp"), P("fsdp", None), P("fsdp", "dp"), P("fsdp", "dp")),
        check_vma=False,
    )
```

```python
import jax
import jax.numpy as jnp
from jax import lax
from jax.experimental import pallas as pl
from jax.experimental.pallas import tpu as pltpu
from jax.sharding import PartitionSpec as P

NS_ITERS = 5

COEF_A = 3.4445
COEF_B = -4.775
COEF_C = 2.0315

MESH = pl.DeviceIdType.MESH
BF16 = jnp.bfloat16
F32 = jnp.float32

N_X = 4
N_DP = 8
N_FSDP = 16
N_CHIPS = N_X * N_FSDP
WIDTHS = (256,) * 7
AHEAD = 2
NORM_EARLY = 3
TAN_PARTS = 4


def dot(left, right):
    return jnp.dot(left, right, preferred_element_type=F32)


def dot_nt(left, right):
    return lax.dot_general(left, right, (((1,), (1,)), ((), ())), preferred_element_type=F32)


def diagonal(shape, row_at, col_at):
    rows = lax.broadcasted_iota(jnp.int32, shape, 0) + row_at
    cols = lax.broadcasted_iota(jnp.int32, shape, 1) + col_at
    return rows == cols


def fold_rows(value):
    rows, cols = value.shape
    part = jnp.sum(value.reshape(rows // 8, 8, cols), axis=0)
    total = part[:, 0:128]
    for at in range(128, cols, 128):
        total = total + part[:, at : at + 128]
    return total


def kernel(
    grad, weight, proj, avg, avg_sq,
    new_weight, moment_one, moment_two, tan_out, gram_out, scale_out,
    own, sib_in, opp_top, opp_bot, from_m, from_p,
    low_part, low_in, low_all, norm_all,
    w_buf, p_buf, m_buf, v_buf, p_bf, p_t, tan_acc,
    tan_send, tan_sib, tan_x, tan_in, tan_all, base_send, base_in, proj_pick, gram_send, gram_in, gram_all, scale_buf,
    load_sem, own_sem, sib_ssem, sib_rsem, x_ssem, x_rsem,
    low_ssem, low_rsem, all_ssem, all_rsem, norm_ssem, norm_rsem, tan_ssem, tan_rsem, tail_ssem, tail_rsem, out_sem,
):
    rows = grad.shape[0]
    rank = proj.shape[1]
    owned = avg.shape[1]
    steps = len(WIDTHS)
    half = rows // 2
    tan_rows = rank // N_DP

    d = lax.axis_index("dp")
    f = lax.axis_index("fsdp")
    x, core = lax.div(d, 2), lax.rem(d, 2)
    y, z = lax.div(f, 4), lax.rem(f, 4)
    xs = [lax.rem(x + i, N_X) for i in range(N_X)]
    ys = [lax.rem(y + i, 4) for i in range(4)]
    zs = [lax.rem(z + i, 4) for i in range(4)]
    far = (2, 1, 3, 0)
    hops = (0, 1, 2, 1)
    sib = {"dp": 2 * x + (1 - core)}
    right = {"dp": 2 * xs[1] + core}
    left = {"dp": 2 * xs[3] + core}

    def remote(src, dst, ssem, rsem, device):
        return pltpu.make_async_remote_copy(
            src_ref=src, dst_ref=dst, send_sem=ssem, recv_sem=rsem, device_id=device, device_id_type=MESH
        )

    def wait_bytes(ref, sem):
        pltpu.make_async_copy(ref, ref, sem).wait()

    planes = sorted(((i, j) for i in range(4) for j in range(4)), key=lambda at: -hops[at[0]] - hops[at[1]])[:-1]
    chips = sorted(
        ((k, i, j) for k in range(4) for i in range(4) for j in range(4)),
        key=lambda at: -hops[at[0]] - hops[at[1]] - hops[at[2]],
    )[:-1]

    def to_fsdp(src_of, dst, ssem, rsem, ordered=False):
        if ordered:
            for i, j in planes:
                to = 4 * ys[i] + zs[j]
                remote(src_of(to), dst, ssem, rsem, {"fsdp": to}).start()
            return

        @pl.loop(1, N_FSDP)
        def _(i):
            to = lax.rem(f + i, N_FSDP)
            remote(src_of(to), dst, ssem, rsem, {"fsdp": to}).start()

    def to_x(src_of, dst, ssem, rsem):
        for i in far[:3]:
            to = xs[i]
            remote(src_of(to), dst, ssem, rsem, {"dp": 2 * to + core}).start()

    def chip_at(at):
        return {"dp": 2 * xs[at[0]] + core, "fsdp": 4 * ys[at[1]] + zs[at[2]]}

    starts = [sum(WIDTHS[:j]) for j in range(steps)]
    cols = [pl.ds(starts[j], WIDTHS[j]) for j in range(steps)]

    def columns(owner, j):
        return pl.ds(pl.multiple_of(owner * owned + starts[j], 128), WIDTHS[j])

    def own_copy(q, j):
        return pltpu.make_async_copy(
            grad.at[:, columns(2 * xs[q] + core, j)], own.at[q, :, cols[j]], own_sem.at[j, q]
        )

    def sib_copy(q, j):
        return remote(
            grad.at[:, columns(2 * xs[q] + (1 - core), j)],
            sib_in.at[q, :, cols[j]], sib_ssem.at[j, q], sib_rsem.at[j, q], sib,
        )

    top, bot = pl.ds(0, half), pl.ds(half, half)

    def x_copy(k, j):
        c = cols[j]
        src, dst, device = (
            (own.at[2, top, c], opp_top.at[:, c], right),
            (own.at[2, bot, c], opp_bot.at[:, c], left),
            (own.at[1, bot, c], from_m.at[bot, c], right),
            (own.at[3, top, c], from_p.at[top, c], left),
            (own.at[1, top, c], from_m.at[top, c], right),
            (own.at[3, bot, c], from_p.at[bot, c], left),
        )[k]
        return remote(src, dst, x_ssem.at[j, k], x_rsem.at[j, k], device)

    loads = [
        pltpu.make_async_copy(proj, p_buf, load_sem.at[0]),
        pltpu.make_async_copy(avg, m_buf, load_sem.at[1]),
        pltpu.make_async_copy(avg_sq, v_buf, load_sem.at[2]),
        pltpu.make_async_copy(weight, w_buf, load_sem.at[3]),
    ]

    def start_loads(j):
        for q in (2, 1, 3, 0):
            own_copy(q, j).start()

    def start_sib(j):
        for q in (2, 1, 3, 0):
            sib_copy(q, j).start()

    loads[0].start()
    start_loads(0)
    barrier = pltpu.get_barrier_semaphore()
    pl.semaphore_signal(barrier, inc=1, device_id=sib, device_id_type=MESH)
    for i in range(1, N_CHIPS):
        to = lax.rem(x * N_FSDP + f + i, N_CHIPS)
        device = {"dp": 2 * lax.div(to, N_FSDP) + core, "fsdp": lax.rem(to, N_FSDP)}
        pl.semaphore_signal(barrier, inc=1, device_id=device, device_id_type=MESH)
    pl.semaphore_wait(barrier, N_CHIPS)

    def pair_sum(q, j):
        own_copy(q, j).wait()
        sib_copy(q, j).wait_recv()
        return own[q, :, cols[j]].astype(F32) + sib_in[q, :, cols[j]].astype(F32)

    def stage_opposite(j):
        own[2, :, cols[j]] = pair_sum(2, j).astype(BF16)
        x_copy(0, j).start()
        x_copy(1, j).start()

    def stage_pair(j):
        own[1, :, cols[j]] = pair_sum(1, j).astype(BF16)
        x_copy(2, j).start()
        own[3, :, cols[j]] = pair_sum(3, j).astype(BF16)
        x_copy(3, j).start()

    def stage_pass(j):
        c = cols[j]
        x_copy(0, j).wait_recv()
        own[1, top, c] = (own[1, top, c].astype(F32) + opp_top[:, c].astype(F32)).astype(BF16)
        x_copy(4, j).start()
        x_copy(1, j).wait_recv()
        own[3, bot, c] = (own[3, bot, c].astype(F32) + opp_bot[:, c].astype(F32)).astype(BF16)
        x_copy(5, j).start()

    def pieces(j):
        if j < steps - 1:
            return [(cols[j], j)]
        part = WIDTHS[j] // 2
        return [(pl.ds(starts[j], part), j), (pl.ds(starts[j] + part, part), steps)]

    def stage_low(j):
        c = cols[j]
        total = pair_sum(0, j)
        for k in (2, 3, 4, 5):
            x_copy(k, j).wait_recv()
        total = (total + from_m[:, c].astype(F32) + from_p[:, c].astype(F32)).astype(BF16)
        own[0, :, c] = total
        low_part[:, :, c] = dot(p_t[...], total).astype(BF16).reshape(N_FSDP, -1, WIDTHS[j])
        for c, k in pieces(j):
            to_fsdp(lambda to: low_part.at[to, :, c], low_in.at[f, :, c], low_ssem.at[k], low_rsem.at[k])

    def stage_adam(j):
        low_in[f, :, cols[j]] = low_part[f, :, cols[j]]
        lows = []
        for c, k in pieces(j):
            wait_bytes(low_in.at[pl.ds(0, N_FSDP - 1), :, c], low_rsem.at[k])
            low = jnp.sum(low_in[:, :, c].astype(F32), axis=0)
            low_all[f, :, c] = low.astype(BF16)
            mine = low_all.at[f, :, c]
            to_fsdp(lambda to: mine, mine, all_ssem.at[k], all_rsem.at[k])
            lows.append(low)
        for low, (c, k) in zip(lows, pieces(j)):
            one = 0.9 * m_buf[:, c] + 0.1 * low
            two = 0.999 * v_buf[:, c] + 0.001 * low * low
            m_buf[:, c] = one
            v_buf[:, c] = two
            norm_all[f, :, c] = (one / (jnp.sqrt(two) + 1e-08)).astype(BF16)

    def stage_norm(j):
        c = cols[j]
        to_fsdp(lambda to: norm_all.at[f, :, c], norm_all.at[f, :, c], norm_ssem.at[j], norm_rsem.at[j])

    def stage_tangent(j):
        for c, k in pieces(j):
            wait_bytes(low_all.at[pl.ds(0, N_FSDP - 1), :, c], all_rsem.at[k])
            low = low_all[:, :, c].reshape(rank, c.size)
            resid = (own[0, :, c].astype(F32) - dot(p_bf[...], low)).astype(BF16)
            if j == 0:
                tan_acc[...] = dot_nt(resid, low)
            else:
                tan_acc[...] += dot_nt(resid, low)

    def weight_copy(j):
        return pltpu.make_async_copy(w_buf.at[:, cols[j]], new_weight.at[:, cols[j]], out_sem.at[j])

    def stage_weight(j):
        c = cols[j]
        wait_bytes(norm_all.at[pl.ds(0, N_FSDP - 1), :, c], norm_rsem.at[j])
        update = dot(p_bf[...], norm_all[:, :, c].reshape(rank, WIDTHS[j]))
        w_buf[:, c] = (w_buf[:, c].astype(F32) - 2.0 * update).astype(BF16)
        weight_copy(j).start()

    pick = diagonal((tan_rows, rank), d * tan_rows, 0).astype(BF16)

    def send_proj_gram():
        proj_pick[...] = dot_nt(pick, p_bf[...]).astype(BF16)
        gram_pp = dot(proj_pick[...], p_bf[...])
        proj_sq = fold_rows(p_buf[...] * p_buf[...])
        proj_sq = jnp.concatenate([proj_sq, jnp.zeros_like(proj_sq)], axis=0).astype(BF16)
        for to_y in range(4):
            for to_z in range(4):
                block = gram_pp[16 * to_y : 16 * to_y + 16, 128 * to_z : 128 * to_z + 128]
                base_send[4 * to_y + to_z, 0:16] = block.astype(BF16)
                base_send[4 * to_y + to_z, 16:32] = proj_sq
        to_fsdp(lambda to: base_send.at[to], base_in.at[f], tail_ssem.at[6], tail_rsem.at[6])
        base_in[f] = base_send[f]

    start_sib(0)
    stage_opposite(0)
    for j in range(1, AHEAD):
        start_loads(j)
        start_sib(j)
    stage_pair(0)
    for copy in loads[1:]:
        copy.start()
    loads[0].wait()
    p_bf[...] = p_buf[...].astype(BF16)
    p_t[...] = dot_nt(diagonal((rank, rank), 0, 0).astype(BF16), p_bf[...]).astype(BF16)

    for t in range(steps + 3):
        if t + AHEAD < steps:
            start_loads(t + AHEAD)
            start_sib(t + AHEAD)
        if t + 1 < steps:
            stage_opposite(t + 1)
        if 0 < t < steps:
            stage_pair(t)
        if t < steps:
            stage_pass(t)
        if t == 1:
            for copy in loads[1:]:
                copy.wait()
            send_proj_gram()
        if 1 <= t < steps + 1:
            stage_low(t - 1)
        if 2 <= t < steps + 2:
            stage_adam(t - 2)
        if 3 <= t:
            stage_tangent(t - 3)
            if t - 3 < NORM_EARLY:
                stage_norm(t - 3)
        if 5 <= t < NORM_EARLY + 5:
            stage_weight(t - 5)

    tan_send[...] = tan_acc[...].astype(BF16).reshape(N_X, 2, tan_rows, rank)
    pair_copy = remote(tan_send.at[:, 1 - core], tan_sib, tail_ssem.at[0], tail_rsem.at[0], sib)
    pair_copy.start()
    stage_norm(NORM_EARLY)
    pair_copy.wait_recv()
    parts = [pl.ds(k * (rank // TAN_PARTS), rank // TAN_PARTS) for k in range(TAN_PARTS)]
    for k, c in enumerate(parts):
        tan_x[:, :, c] = (tan_send[:, core, :, c].astype(F32) + tan_sib[:, :, c].astype(F32)).astype(BF16)
        to_x(lambda to: tan_x.at[to, :, c], tan_in.at[x, :, c], tan_ssem.at[0, k], tan_rsem.at[0, k])
        tan_in[x, :, c] = tan_x[x, :, c]
    for j in range(NORM_EARLY + 1, steps - 1):
        stage_norm(j)
    for k, c in enumerate(parts):
        wait_bytes(tan_in.at[pl.ds(0, N_X - 1), :, c], tan_rsem.at[0, k])
        tan_all[x, core, :, c] = jnp.sum(tan_in[:, :, c].astype(F32), axis=0).astype(BF16)
        mine = tan_all.at[x, core, :, c]
        to_x(lambda to: mine, mine, tan_ssem.at[1, k], tan_rsem.at[1, k])
    stage_norm(steps - 1)
    outs = [
        pltpu.make_async_copy(m_buf, moment_one, out_sem.at[steps]),
        pltpu.make_async_copy(v_buf, moment_two, out_sem.at[steps + 1]),
    ]
    for copy in outs:
        copy.start()
    for j in range(NORM_EARLY, NORM_EARLY + 2):
        stage_weight(j)
    pair_all = []
    for k, c in enumerate(parts):
        wait_bytes(tan_all.at[pl.ds(0, N_X - 1), 0, :, c], tan_rsem.at[1, k])
        mine = tan_all.at[:, core, :, c]
        pair_all.append(remote(mine, mine, tan_ssem.at[2, k], tan_rsem.at[2, k], sib))
        pair_all[k].start()
    for copy in pair_all:
        copy.wait_recv()

    tan = tan_all[...].reshape(rank, rank)
    tan_copy = pltpu.make_async_copy(tan_all, tan_out, out_sem.at[steps + 2])
    tan_copy.start()
    tan_pick = dot_nt(pick, tan).astype(BF16)
    with_tan = dot(jnp.concatenate([proj_pick[...], tan_pick], axis=0), tan)
    gram_pt = dot(tan_pick, p_bf[...]) + with_tan[:tan_rows]
    gram_tt = with_tan[tan_rows:]
    tan_f = tan.astype(F32)
    tan_sq = fold_rows(tan_f * tan_f)
    stats = jnp.concatenate([tan_sq, jnp.zeros_like(tan_sq)], axis=0).astype(BF16)
    for to_y in range(4):
        for to_z in range(4):
            block = (slice(16 * to_y, 16 * to_y + 16), slice(128 * to_z, 128 * to_z + 128))
            at = 4 * to_y + to_z
            gram_send[at, 0:16] = gram_pt[block].astype(BF16)
            gram_send[at, 16:32] = gram_tt[block].astype(BF16)
            gram_send[at, 32:48] = stats
    to_fsdp(lambda to: gram_send.at[to], gram_in.at[f], tail_ssem.at[4], tail_rsem.at[4], True)
    gram_in[f] = gram_send[f]
    for j in range(NORM_EARLY + 2, steps):
        stage_weight(j)
    for j in range(steps):
        c = cols[j]
        for q in range(N_X):
            sib_copy(q, j).wait_send()
        for k in range(6):
            x_copy(k, j).wait_send()
        for part, k in pieces(j):
            wait_bytes(low_in.at[pl.ds(0, N_FSDP - 1), :, part], low_ssem.at[k])
            wait_bytes(low_all.at[pl.ds(0, N_FSDP - 1), :, part], all_ssem.at[k])
        wait_bytes(norm_all.at[pl.ds(0, N_FSDP - 1), :, c], norm_ssem.at[j])
    wait_bytes(base_in.at[pl.ds(0, N_FSDP - 1)], tail_rsem.at[6])
    base = jnp.sum(base_in[...].astype(F32), axis=0)
    proj_total = jnp.sum(base[16:32])
    wait_bytes(gram_in.at[pl.ds(0, N_FSDP - 1)], tail_rsem.at[4])
    sums = jnp.sum(gram_in[...].astype(F32), axis=0)
    tan_total = jnp.sum(sums[32:40])
    tan_scale = 0.5 * jnp.sqrt(F32(rank)) / jnp.sqrt(jnp.full((1, 1), tan_total, F32) + 1e-06)
    middle = (proj_total + tan_scale * tan_scale * tan_total) / rank
    block = base[0:16] + tan_scale * sums[0:16] + tan_scale * tan_scale * sums[16:32]
    on_diagonal = diagonal((16, 128), d * tan_rows + y * 16, z * 128)
    gram_all[x, core, f] = (block - jnp.where(on_diagonal, middle, 0.0)).astype(BF16)
    mine = gram_all.at[x, core, f]

    for at in chips:
        remote(mine, mine, tail_ssem.at[5], tail_rsem.at[5], chip_at(at)).start()

    scale_buf[0:8] = jnp.broadcast_to(tan_scale, (8, 128))
    scale_buf[8:16] = jnp.broadcast_to(middle, (8, 128))
    scale_copy = pltpu.make_async_copy(scale_buf, scale_out, out_sem.at[steps + 3])
    scale_copy.start()
    wait_bytes(base_in.at[pl.ds(0, N_FSDP - 1)], tail_ssem.at[6])
    pair_copy.wait_send()
    for k, c in enumerate(parts):
        wait_bytes(tan_in.at[pl.ds(0, N_X - 1), :, c], tan_ssem.at[0, k])
        wait_bytes(tan_all.at[pl.ds(0, N_X - 1), 0, :, c], tan_ssem.at[1, k])
        pair_all[k].wait_send()
    wait_bytes(gram_in.at[pl.ds(0, N_FSDP - 1)], tail_ssem.at[4])
    for copy in outs:
        copy.wait()
    for j in range(steps):
        weight_copy(j).wait()
    tan_copy.wait()
    blocks = own.at[0, pl.ds(0, 144), pl.ds(0, 896)]
    wait_bytes(blocks, tail_rsem.at[5])
    pair_gram = remote(gram_all.at[:, core], gram_all.at[:, core], tail_ssem.at[7], tail_rsem.at[7], sib)
    pair_gram.start()
    pair_gram.wait_recv()
    gram_copy = pltpu.make_async_copy(gram_all, gram_out, out_sem.at[steps + 4])
    gram_copy.start()

    wait_bytes(blocks, tail_ssem.at[5])
    pair_gram.wait_send()
    scale_copy.wait()
    gram_copy.wait()


def finish_kernel(
    weight_in, one_in, two_in, tan, gram, scale, proj,
    new_weight, new_proj, moment_one, moment_two,
    tan_buf, gram_buf, scale_buf, proj_buf, w_state, q_state, out_buf, weight_buf, one_buf, two_buf, sems,
):
    rank = proj.shape[1]
    copies = [
        pltpu.make_async_copy(gram, gram_buf, sems.at[0]),
        pltpu.make_async_copy(scale, scale_buf, sems.at[1]),
        pltpu.make_async_copy(tan, tan_buf, sems.at[2]),
        pltpu.make_async_copy(proj, proj_buf, sems.at[3]),
        pltpu.make_async_copy(weight_in, weight_buf, sems.at[4]),
        pltpu.make_async_copy(one_in, one_buf, sems.at[5]),
        pltpu.make_async_copy(two_in, two_buf, sems.at[6]),
    ]
    passed = [
        pltpu.make_async_copy(weight_buf, new_weight, sems.at[4]),
        pltpu.make_async_copy(one_buf, moment_one, sems.at[5]),
        pltpu.make_async_copy(two_buf, moment_two, sems.at[6]),
    ]
    for copy in copies:
        copy.start()
    copies[0].wait()
    copies[1].wait()
    tan_scale = scale_buf[0:1, 0:1]
    middle = scale_buf[8:9, 0:1]
    eye = diagonal((rank, rank), 0, 0)
    whole = gram_buf[...].astype(F32).reshape(N_DP, 4, 4, 16, 128)
    gram_dev = jnp.concatenate([whole[:, :, at].reshape(rank, 128) for at in range(4)], axis=1)
    trace_dev = jnp.sum(jnp.sum(jnp.where(eye, gram_dev, 0.0), axis=0, keepdims=True), axis=1, keepdims=True)
    frame_sq = trace_dev + rank * middle + 1e-06
    inverse = 1.0 / frame_sq
    shift = trace_dev / rank
    center = (middle + shift) * inverse
    state = (gram_dev - jnp.where(eye, shift, 0.0)) * inverse
    w_state[...] = state
    q_center = None
    for sweep in range(NS_ITERS):
        state = w_state[...]
        state_b = state.astype(BF16)
        poly = (COEF_B + 2.0 * COEF_C * center) * state + COEF_C * dot(state_b, state_b)
        poly_center = COEF_A + COEF_B * center + COEF_C * center * center
        poly_b = poly.astype(BF16)
        if sweep == 0:
            q_state[...] = poly
            q_center = poly_center
        else:
            q_now = q_state[...]
            q_state[...] = q_center * poly + poly_center * q_now + dot(q_now.astype(BF16), poly_b)
            q_center = q_center * poly_center
        if sweep == 1:
            for copy, on in zip(copies[4:], passed):
                copy.wait()
                on.start()
        if sweep < NS_ITERS - 1:
            once = center * poly + poly_center * state + dot(state_b, poly_b)
            once_center = center * poly_center
            w_state[...] = once_center * poly + poly_center * once + dot(once.astype(BF16), poly_b)
            center = once_center * poly_center
    q_now = q_state[...]
    q_shift = jnp.sum(jnp.sum(jnp.where(eye, q_now, 0.0), axis=0, keepdims=True), axis=1, keepdims=True) / rank
    q_b = (q_now - jnp.where(eye, q_shift, 0.0)).astype(BF16)
    copies[2].wait()
    copies[3].wait()
    scale_down = 1.0 / jnp.sqrt(frame_sq)
    q_all = q_center + q_shift
    last = []
    part = proj_buf.shape[0] // N_X
    for k in range(N_X):
        at = pl.ds(k * part, part)
        frame = (proj_buf[at] + tan_scale * tan_buf[k].reshape(part, rank).astype(F32)) * scale_down
        out_buf[at] = q_all * frame + dot(frame.astype(BF16), q_b)
        last.append(pltpu.make_async_copy(out_buf.at[at], new_proj.at[at], sems.at[7 + k]))
        last[k].start()
    for copy in passed:
        copy.wait()
    for copy in last:
        copy.wait()


def on_device(grad_parts, weight, projector, exp_avg, exp_avg_sq):
    grad = grad_parts.reshape(grad_parts.shape[1:])
    rows = grad.shape[0]
    rank = projector.shape[1]
    share, owned = exp_avg.shape
    steps = len(WIDTHS)
    tan_rows = rank // N_DP
    vmem = pltpu.VMEM
    dma = pltpu.SemaphoreType.DMA
    hbm = pl.BlockSpec(memory_space=pl.ANY)
    shape = jax.ShapeDtypeStruct
    tan_shape = (N_X, 2, tan_rows, rank)
    gram_shape = (N_X, 2, N_FSDP, 16, 128)
    mid = pl.pallas_call(
        kernel,
        out_shape=(
            shape(weight.shape, weight.dtype),
            shape(exp_avg.shape, F32),
            shape(exp_avg_sq.shape, F32),
            shape(tan_shape, BF16),
            shape(gram_shape, BF16),
            shape((16, 128), F32),
        ),
        in_specs=[hbm] * 5,
        out_specs=(hbm,) * 6,
        scratch_shapes=[
            vmem((N_X, rows, owned), BF16),
            vmem((N_X, rows, owned), BF16),
            vmem((rows // 2, owned), BF16),
            vmem((rows // 2, owned), BF16),
            vmem((rows, owned), BF16),
            vmem((rows, owned), BF16),
            vmem((N_FSDP, share, owned), BF16),
            vmem((N_FSDP, share, owned), BF16),
            vmem((N_FSDP, share, owned), BF16),
            vmem((N_FSDP, share, owned), BF16),
            vmem(weight.shape, BF16),
            vmem(projector.shape, F32),
            vmem(exp_avg.shape, F32),
            vmem(exp_avg_sq.shape, F32),
            vmem(projector.shape, BF16),
            vmem((rank, rows), BF16),
            vmem((rows, rank), F32),
            vmem(tan_shape, BF16),
            vmem((N_X, tan_rows, rank), BF16),
            vmem((N_X, tan_rows, rank), BF16),
            vmem((N_X, tan_rows, rank), BF16),
            vmem(tan_shape, BF16),
            vmem((N_FSDP, 32, 128), BF16),
            vmem((N_FSDP, 32, 128), BF16),
            vmem((tan_rows, rank), BF16),
            vmem((N_FSDP, 48, 128), BF16),
            vmem((N_FSDP, 48, 128), BF16),
            vmem(gram_shape, BF16),
            vmem((16, 128), F32),
            dma((4,)),
            dma((steps, N_X)),
            dma((steps, N_X)),
            dma((steps, N_X)),
            dma((steps, 6)),
            dma((steps, 6)),
            dma((steps + 1,)),
            dma((steps + 1,)),
            dma((steps + 1,)),
            dma((steps + 1,)),
            dma((steps,)),
            dma((steps,)),
            dma((3, TAN_PARTS)),
            dma((3, TAN_PARTS)),
            dma((8,)),
            dma((8,)),
            dma((steps + 5,)),
        ],
        compiler_params=pltpu.CompilerParams(
            collective_id=0, has_side_effects=True, vmem_limit_bytes=60 * 1024 * 1024
        ),
    )(grad, weight, projector, exp_avg, exp_avg_sq)
    return pl.pallas_call(
        finish_kernel,
        out_shape=(
            shape(weight.shape, weight.dtype),
            shape(projector.shape, F32),
            shape(exp_avg.shape, F32),
            shape(exp_avg_sq.shape, F32),
        ),
        in_specs=[hbm] * 7,
        out_specs=(hbm,) * 4,
        scratch_shapes=[
            vmem(tan_shape, BF16),
            vmem(gram_shape, BF16),
            vmem((16, 128), F32),
            vmem(projector.shape, F32),
            vmem((rank, rank), F32),
            vmem((rank, rank), F32),
            vmem(projector.shape, F32),
            vmem(weight.shape, BF16),
            vmem(exp_avg.shape, F32),
            vmem(exp_avg_sq.shape, F32),
            dma((11,)),
        ],
        compiler_params=pltpu.CompilerParams(vmem_limit_bytes=60 * 1024 * 1024),
    )(*mid, projector)


def solution(mesh):
    return jax.shard_map(
        on_device,
        mesh=mesh,
        in_specs=(
            P("dp", "fsdp", None),
            P("fsdp", "dp"),
            P("fsdp", None),
            P("fsdp", "dp"),
            P("fsdp", "dp"),
        ),
        out_specs=(P("fsdp", "dp"), P("fsdp", None), P("fsdp", "dp"), P("fsdp", "dp")),
        check_vma=False,
    )
```
